256 devices in a mesh: ctx: 8 (over y, core), chan: 32 (over x, z).
Axes of the slice: x: 4, y: 4, z: 8, core: 2. Of those that a mesh axis runs over, the one named last changes fastest.
Arguments:
- query: bfloat16 [8192, 8192], P('ctx', 'chan'), may hold values from -6 to 6
- key: bfloat16 [8192, 8192], P('ctx', 'chan'), may hold values from -6 to 6
- value: bfloat16 [8192, 8192], P('ctx', 'chan'), may hold values from -6 to 6
- out_grad: bfloat16 [8192, 8192], P('ctx', 'chan'), may hold values from -6 to 6
- out_weight: bfloat16 [8192, 8192], P(None, 'chan'), may hold values from -0.0625 to 0.0625
- rate: float32 [512, 16], P('chan'), may hold values from 2.4414063e-05 to 0.05, as said below
- residue: float32 [512, 16], P('chan'), may hold values from -0.2 to 0.2
Outputs:
- d_query: bfloat16 [8192, 8192], P('ctx', 'chan')
- d_key: bfloat16 [8192, 8192], P('ctx', 'chan')
- d_value: bfloat16 [8192, 8192], P('ctx', 'chan')
- d_weight: float32 [8192, 8192], P('ctx', 'chan')
- d_residue: float32 [512, 16], P('chan')
- d_rate: float32 [512, 16], P('chan')
The draws below stay inside these ranges and needn't reach their ends.
Inputs may be any that keep to these rules, and one draw needn't show every extreme that they name: `rate`: decay rates of the modes.
All inputs are finite; a program needn't handle non-finite values.
Results may differ from the reference program's by a relative error of at most 0.017.
Values may be sent and summed in bfloat16 or wider, within the bound.
No kernel may reach another device: no remote copies, remote signals or barrier semaphores. Data moves between devices by JAX's collectives and lax.ppermute only.
A program may use at most 128 MiB of HBM per device.

```python
import jax
import jax.numpy as jnp
from jax import lax

D = 8192
GROUP = 16
POLES = 16
TOKENS = 8192
GROUPS = 512


def draw_rate(key, part):
    key = jax.random.fold_in(key, 7)
    pick_key, slow_key, fast_key = jax.random.split(key, 3)
    share = 0.5
    slow = jnp.exp(jax.random.uniform(slow_key, (GROUPS, POLES), jnp.float32, jnp.log(0.2 / TOKENS), jnp.log(2.0 / TOKENS)))
    fast = jnp.exp(jax.random.uniform(fast_key, (GROUPS, POLES), jnp.float32, jnp.log(0.02), jnp.log(0.05)))
    picks = jax.random.uniform(pick_key, (GROUPS, POLES), jnp.float32)
    return jnp.where(picks < share, slow, fast).astype(jnp.float32)


def level_of(own_key, extent, cuts, smallest, top_value):
    gain, own = 1.0, jax.random.fold_in(own_key, 6)
    for axis_at, parts in cuts:
        steps = jnp.exp(jax.random.uniform(jax.random.fold_in(own, axis_at), (parts,), jnp.float32, smallest / len(cuts), top_value / len(cuts)))
        gain = gain * jnp.repeat(steps, extent[axis_at] // parts).reshape([-1 if axis == axis_at else 1 for axis in range(len(extent))])
    return gain


def noise(rng, extent, width, reach, cuts=(), dtype=jnp.bfloat16):
    values = jax.random.normal(rng, extent, jnp.float32) * width
    if len(cuts) > 0:
        values = level_of(rng, extent, cuts, -0.22, 0.18) * values
    return jnp.clip(values, min=-reach, max=reach).astype(dtype)


def setup_inputs(seed: int = 0) -> dict:
    seeds = jax.random.split(jax.random.key(seed), 8)
    return {
        "query": noise(seeds[0], (TOKENS, D), 1.0, 6.0, ((0, 8), (1, 32))),
        "key": noise(seeds[1], (TOKENS, D), 1.0, 6.0, ((0, 8), (1, 32))),
        "value": noise(seeds[2], (TOKENS, D), 1.0, 6.0, ((0, 8), (1, 32))),
        "out_grad": noise(seeds[3], (TOKENS, D), 1.0, 6.0, ((0, 8), (1, 32))),
        "out_weight": noise(seeds[4], (D, D), D ** -0.5, 0.0625, ((1, 32),)),
        "rate": draw_rate(jax.random.fold_in(seeds[7], 71), 0),
        "residue": noise(seeds[6], (GROUPS, POLES), 0.02, 0.2, ((0, 32),), jnp.float32),
    }


def reference(query, key, value, out_grad, out_weight, rate, residue):
    grad_mid = jnp.dot(out_grad, out_weight, preferred_element_type=jnp.float32).astype(jnp.bfloat16)
    inner = key.astype(jnp.float32) * value.astype(jnp.float32)
    grad_conv = grad_mid.astype(jnp.float32) * query.astype(jnp.float32)
    decay_chan = jnp.repeat(jnp.exp(-rate).T, GROUP, axis=1)
    weight_chan = jnp.repeat(residue.T, GROUP, axis=1)
    zero_state = jnp.zeros((POLES, D), jnp.float32)

    def forward_step(carry, items):
        state, slope, acc_res, acc_rate = carry
        inner_row, grad_row = items
        slope = decay_chan * (slope + state)
        state = decay_chan * state + inner_row[None, :]
        conv_row = jnp.sum(weight_chan * state, axis=0)
        acc_res = acc_res + grad_row[None, :] * state
        acc_rate = acc_rate + grad_row[None, :] * slope
        return (state, slope, acc_res, acc_rate), conv_row

    carry, conv = lax.scan(forward_step, (zero_state, zero_state, zero_state, zero_state), (inner, grad_conv))
    acc_res, acc_rate = carry[2], carry[3]

    def backward_step(state, grad_row):
        state = decay_chan * state + grad_row[None, :]
        return state, jnp.sum(weight_chan * state, axis=0)

    final_state, back = lax.scan(backward_step, zero_state, grad_conv, reverse=True)
    d_query = (grad_mid.astype(jnp.float32) * conv).astype(jnp.bfloat16)
    gated = (query.astype(jnp.float32) * conv).astype(jnp.bfloat16)
    d_key = (back * value.astype(jnp.float32)).astype(jnp.bfloat16)
    d_value = (back * key.astype(jnp.float32)).astype(jnp.bfloat16)
    scale = 1.0 / TOKENS
    d_residue = acc_res.reshape(POLES, GROUPS, GROUP).sum(axis=2).T * scale
    d_rate = -residue * acc_rate.reshape(POLES, GROUPS, GROUP).sum(axis=2).T * scale
    d_weight = jnp.dot(out_grad.T, gated, preferred_element_type=jnp.float32) * scale
    return d_query, d_key, d_value, d_weight, d_residue, d_rate
```

```python
import functools

import jax
import jax.numpy as jnp
from jax import lax
from jax.experimental import pallas as pl
from jax.experimental.pallas import tpu as pltpu
from jax.sharding import Mesh
from jax.sharding import PartitionSpec as P

BLK = 128
F32 = jnp.float32
BF16 = jnp.bfloat16
VMEM_LIMIT = 56 * 1024 * 1024
CTX = ("y", "core")
CHAN = ("x", "z")


def split(x):
    hi = x.astype(BF16)
    return hi, (x - hi.astype(F32)).astype(BF16)


def mm(a, b, ca=1, cb=0):
    return lax.dot_general(a, b, (((ca,), (cb,)), ((), ())), preferred_element_type=F32)


def lanes(shape):
    return lax.broadcasted_iota(jnp.int32, shape, 1).astype(F32)


def rows(shape):
    return lax.broadcasted_iota(jnp.int32, shape, 0).astype(F32)


def stacked(ref, g, width, blocks):
    return jnp.concatenate(
        [ref[g * width : (g + 1) * width, b * BLK : (b + 1) * BLK] for b in range(blocks)], axis=0
    )


def with_states(x, taps, state, lead_hi, lead_lo):
    poles = lead_hi.shape[0]
    none = jnp.zeros((BLK - poles, BLK), BF16)
    s_hi, s_lo = split(state)
    first = mm(
        jnp.concatenate([x, s_hi], axis=1), jnp.concatenate([taps, lead_hi, none], axis=0)
    )
    second = mm(
        jnp.concatenate([s_lo, s_hi], axis=1),
        jnp.concatenate([lead_hi, none, lead_lo, none], axis=0),
    )
    return first + second


def sums_rhs(top, second, third, fourth):
    poles = top[0].shape[0]
    none = jnp.zeros((poles, 2 * BLK), BF16)
    rest = jnp.zeros((BLK - 2 * poles, 2 * BLK), BF16)

    def part(pair):
        return none if pair is None else jnp.concatenate(pair, axis=1)

    return jnp.concatenate(
        [part(top), part(second), rest, part(third), part(fourth), rest], axis=0
    )


def forward_kernel(
    key_ref, value_ref, rate_col_ref, res_col_ref, rate_two_ref, conv_ref, ends_ref, xt_ref, states_ref, ct_ref, sums_ref, fin_ref
):
    tokens, channels = key_ref.shape
    groups, poles = rate_two_ref.shape[0], rate_col_ref.shape[0] // rate_two_ref.shape[0]
    width, blocks = channels // groups, tokens // BLK
    for b in range(blocks):
        at = slice(b * BLK, (b + 1) * BLK)
        inner = key_ref[at, :].astype(F32) * value_ref[at, :].astype(F32)
        xt_ref[:, at] = inner.T.astype(BF16)
    rate, res = rate_col_ref[...], res_col_ref[...]
    time = lanes(rate.shape)
    u_hi, u_lo = split(res * jnp.exp(-rate * (time - 64.0)))
    v_hi, v_lo = split(jnp.exp(rate * (time - 64.0)))
    tail_all = jnp.exp(-rate * (BLK - 1.0 - time))
    tail = split(tail_all)
    tail_lag = split((BLK - 1.0 - time) * tail_all)
    lead = split(res * jnp.exp(-rate * (time + 1.0)))
    for g in range(groups):
        own = slice(g * poles, (g + 1) * poles)
        x = stacked(xt_ref, g, width, blocks)
        top = tuple(part[own] for part in tail)
        lag = tuple(part[own] for part in tail_lag)
        sums_ref[g] = mm(
            jnp.concatenate([x, x], axis=1), sums_rhs(top, lag, None, top), 1, 1
        )
    span = jnp.exp(-float(BLK) * rate_two_ref[...])
    lane = lanes((1, BLK))
    for g in range(groups):
        step = span[g : g + 1, :]
        couple = jnp.where(lane >= poles, float(BLK) * step, 0.0)
        state = jnp.zeros((width, BLK), F32)
        twin = jnp.zeros((width, BLK), F32)
        for b in range(blocks):
            at = slice(b * width, (b + 1) * width)
            states_ref[g, at, :] = state
            state = step * state + couple * twin + sums_ref[g, at, :BLK]
            twin = step * twin + sums_ref[g, at, BLK:]
        fin_ref[g * width : (g + 1) * width, :] = state
    ends_ref[...] = fin_ref[...].T[: 2 * poles, :]
    causal = lanes((BLK, BLK)) >= rows((BLK, BLK))
    for g in range(groups):
        own = slice(g * poles, (g + 1) * poles)
        x = stacked(xt_ref, g, width, blocks)
        taps = mm(
            jnp.concatenate([v_hi[own], v_lo[own], v_hi[own]], axis=0),
            jnp.concatenate([u_hi[own], u_hi[own], u_lo[own]], axis=0),
            0,
            0,
        )
        taps = jnp.where(causal, taps, 0.0).astype(BF16)
        out = with_states(x, taps, states_ref[g], lead[0][own], lead[1][own])
        for b in range(blocks):
            ct_ref[g * width : (g + 1) * width, b * BLK : (b + 1) * BLK] = out[
                b * width : (b + 1) * width
            ]
    for b in range(blocks):
        at = slice(b * BLK, (b + 1) * BLK)
        conv_ref[at, :] = ct_ref[:, at].T


def spread(state, groups):
    poles, channels = state.shape
    width = channels // groups
    tall = jnp.concatenate([state] * groups, axis=0)
    row = lax.broadcasted_iota(jnp.int32, tall.shape, 0) // poles
    col = lax.broadcasted_iota(jnp.int32, tall.shape, 1) // width
    return jnp.where(row == col, tall, 0.0)


def modes(lead, state_tall):
    l_hi, l_lo = split(lead)
    s_hi, s_lo = split(state_tall)
    return mm(l_hi, s_hi) + mm(l_hi, s_lo) + mm(l_lo, s_hi)


def enter_kernel(
    mine_ref, all_ref, conv_ref, query_ref, rate_row_ref, res_row_ref, rate_nc_ref, conv_out_ref, gated_ref, in_ref
):
    tokens, channels = conv_ref.shape
    poles = rate_nc_ref.shape[0]
    groups = rate_row_ref.shape[1] // poles
    mine = mine_ref[0]
    count = all_ref.shape[0]
    rate_nc = rate_nc_ref[...]
    state = jnp.zeros((poles, channels), F32)
    slope = jnp.zeros((poles, channels), F32)
    for i in range(count - 1):
        gap = (mine - 1 - i).astype(F32)
        lag = jnp.maximum(gap, 0.0) * float(tokens)
        weight = jnp.where(gap >= 0.0, jnp.exp(-rate_nc * lag), 0.0)
        end = all_ref[i, :poles, :]
        state = state + weight * end
        slope = slope + weight * (all_ref[i, poles:, :] + lag * end)
    in_ref[:poles, :] = state
    in_ref[poles:, :] = slope
    tall = spread(state, groups)
    for b in range(tokens // BLK):
        at = slice(b * BLK, (b + 1) * BLK)
        time = rows((BLK, rate_row_ref.shape[1])) + float(b * BLK + 1)
        lead = res_row_ref[...] * jnp.exp(-rate_row_ref[...] * time)
        conv = conv_ref[at, :] + modes(lead, tall)
        conv_out_ref[at, :] = conv
        gated_ref[at, :] = (query_ref[at, :].astype(F32) * conv).astype(BF16)


def backward_kernel(
    own_ref, p1_ref, p2_ref, p3_ref, query_ref, conv_ref, xt_ref, states_ref, in_ref, rate_col_ref, res_col_ref, rate_two_ref,
    rate_nc_ref, dq_ref, back_ref, pay_ref, gt_ref, bt_ref, sums_ref, rs_ref, fin_ref, cross_ref
):
    tokens, channels = query_ref.shape
    groups, poles = rate_two_ref.shape[0], rate_nc_ref.shape[0]
    width, blocks = channels // groups, tokens // BLK
    for b in range(blocks):
        at = slice(b * BLK, (b + 1) * BLK)
        total = (own_ref[at, :].astype(F32) + p1_ref[at, :].astype(F32)) + (
            p2_ref[at, :].astype(F32) + p3_ref[at, :].astype(F32)
        )
        grad = total.astype(BF16).astype(F32)
        dq_ref[at, :] = (grad * conv_ref[at, :]).astype(BF16)
        gt_ref[:, at] = (grad * query_ref[at, :].astype(F32)).T.astype(BF16)
    rate, res = rate_col_ref[...], res_col_ref[...]
    time = lanes(rate.shape)
    u_hi, u_lo = split(res * jnp.exp(-rate * (time - 64.0)))
    v_all = jnp.exp(rate * (time - 64.0))
    v_hi, v_lo = split(v_all)
    w_hi, w_lo = split((time - 64.0) * v_all)
    head_all = jnp.exp(-rate * time)
    head = split(head_all)
    head_lag = split(time * head_all)
    trail = split(res * jnp.exp(-rate * (BLK - time)))
    for g in range(groups):
        own = slice(g * poles, (g + 1) * poles)
        y = stacked(gt_ref, g, width, blocks)
        top = tuple(part[own] for part in head)
        lag = tuple(part[own] for part in head_lag)
        sums_ref[g] = mm(jnp.concatenate([y, y], axis=1), sums_rhs(top, lag, lag, top), 1, 1)
    span = jnp.exp(-float(BLK) * rate_two_ref[...])
    lane = lanes((1, BLK))
    low = lane < poles
    for g in range(groups):
        step = span[g : g + 1, :]
        couple = jnp.where(lane >= poles, float(BLK) * step, 0.0)
        state = jnp.zeros((width, BLK), F32)
        twin = jnp.zeros((width, BLK), F32)
        res_sum = jnp.zeros((width, BLK), F32)
        rate_sum = jnp.zeros((width, BLK), F32)
        for b in reversed(range(blocks)):
            at = slice(b * width, (b + 1) * width)
            rs_ref[g, at, :] = state
            first, second = sums_ref[g, at, :BLK], sums_ref[g, at, BLK:]
            before = states_ref[g, at, :]
            res_sum = res_sum + jnp.where(low, first * before, 0.0)
            rate_sum = rate_sum + (second + jnp.where(low, first, 0.0)) * before
            state, twin = (
                step * state + couple * twin + first,
                step * twin + jnp.where(low, 0.0, second),
            )
        fin_ref[g * width : (g + 1) * width, :] = state
        decay = jnp.exp(-rate_two_ref[g : g + 1, :])
        cross_ref[0, g * width : (g + 1) * width, :] = decay * res_sum
        cross_ref[1, g * width : (g + 1) * width, :] = decay * rate_sum
    causal = rows((BLK, BLK)) >= lanes((BLK, BLK))
    for g in range(groups):
        own = slice(g * poles, (g + 1) * poles)
        y = stacked(gt_ref, g, width, blocks)
        taps = mm(
            jnp.concatenate([u_hi[own], u_hi[own], u_lo[own]], axis=0),
            jnp.concatenate([v_hi[own], v_lo[own], v_hi[own]], axis=0),
            0,
            0,
        )
        taps = jnp.where(causal, taps, 0.0).astype(BF16)
        out = with_states(y, taps, rs_ref[g], trail[0][own], trail[1][own])
        for b in range(blocks):
            bt_ref[g * width : (g + 1) * width, b * BLK : (b + 1) * BLK] = out[
                b * width : (b + 1) * width
            ]
        x = stacked(xt_ref, g, width, blocks)
        pairs = jnp.where(causal, mm(y, x, 0, 0), 0.0).astype(BF16)
        rhs = jnp.concatenate(
            [
                jnp.concatenate([v_hi[own], v_lo[own]], axis=1),
                jnp.concatenate([w_hi[own], w_lo[own]], axis=1),
                jnp.zeros((BLK - 2 * poles, 2 * BLK), BF16),
            ],
            axis=0,
        )
        held = mm(jnp.concatenate([pairs, pairs], axis=1), rhs, 1, 1)
        since = rows((BLK, BLK)) - 64.0
        held = held * jnp.exp(-rate_two_ref[g : g + 1, :] * since)
        res_row = jnp.sum(jnp.where(low, held, 0.0), axis=0, keepdims=True)
        rate_row = jnp.sum(jnp.where(low, since * held, -held), axis=0, keepdims=True)
        one = slice(g * width, g * width + 1)
        cross_ref[0, one, :] = cross_ref[0, one, :] + res_row
        cross_ref[1, one, :] = cross_ref[1, one, :] + rate_row
    starts = fin_ref[...].T
    start, start_lag = starts[:poles], starts[poles : 2 * poles]
    state_in, slope_in = in_ref[:poles, :], in_ref[poles:, :]
    decay = jnp.exp(-rate_nc_ref[...])
    res_cross = cross_ref[0].T[:poles]
    rate_cross = cross_ref[1].T
    pay_ref[:poles, :] = start
    pay_ref[poles : 2 * poles, :] = res_cross + decay * start * state_in
    pay_ref[2 * poles :, :] = (
        rate_cross[:poles]
        + rate_cross[poles : 2 * poles]
        + decay * ((start_lag + start) * state_in + start * slope_in)
    )
    for b in range(blocks):
        at = slice(b * BLK, (b + 1) * BLK)
        back_ref[at, :] = bt_ref[:, at].T


def leave_kernel(
    mine_ref, all_ref, back_ref, key_ref, value_ref, rate_row_ref, res_row_ref, rate_nc_ref, res_ref, dk_ref, dv_ref, dres_ref, drate_ref
):
    tokens, channels = back_ref.shape
    poles = rate_nc_ref.shape[0]
    groups = rate_row_ref.shape[1] // poles
    mine = mine_ref[0]
    count = all_ref.shape[0]
    rate_nc = rate_nc_ref[...]
    state = jnp.zeros((poles, channels), F32)
    for i in range(1, count):
        gap = (i - 1 - mine).astype(F32)
        lag = jnp.maximum(gap, 0.0) * float(tokens)
        weight = jnp.where(gap >= 0.0, jnp.exp(-rate_nc * lag), 0.0)
        state = state + weight * all_ref[i, :poles, :]
    tall = spread(state, groups)
    total = all_ref[0, poles:, :]
    for i in range(1, count):
        total = total + all_ref[i, poles:, :]
    scale = 1.0 / float(tokens * count)
    width = channels // groups
    shape = (groups, channels)
    ind = (
        lax.broadcasted_iota(jnp.int32, shape, 0)
        == lax.broadcasted_iota(jnp.int32, shape, 1) // width
    ).astype(F32)
    both = lax.dot_general(
        ind, total, (((1,), (1,)), ((), ())), preferred_element_type=F32, precision=lax.Precision.HIGHEST
    )
    dres_ref[...] = both[:, :poles] * scale
    drate_ref[...] = -res_ref[...] * both[:, poles:] * scale
    for b in range(tokens // BLK):
        at = slice(b * BLK, (b + 1) * BLK)
        time = float(tokens - b * BLK) - rows((BLK, rate_row_ref.shape[1]))
        trail = res_row_ref[...] * jnp.exp(-rate_row_ref[...] * time)
        back = back_ref[at, :] + modes(trail, tall)
        dk_ref[at, :] = (back * value_ref[at, :].astype(F32)).astype(BF16)
        dv_ref[at, :] = (back * key_ref[at, :].astype(F32)).astype(BF16)


def call(kernel, outs, scratch, ops, scalars=0, flops=10**9):
    spec = pl.BlockSpec(memory_space=pltpu.VMEM)
    return pl.pallas_call(
        kernel,
        out_shape=outs,
        in_specs=[pl.BlockSpec(memory_space=pltpu.SMEM)] * scalars + [spec] * (len(ops) - scalars),
        out_specs=[spec] * len(outs),
        scratch_shapes=scratch,
        compiler_params=pltpu.CompilerParams(vmem_limit_bytes=VMEM_LIMIT),
        cost_estimate=pl.CostEstimate(flops=flops, bytes_accessed=4 * 2**20, transcendentals=0),
    )(*ops)


def shift(n, by):
    return [(i, (i + by) % n) for i in range(n)]


def gather_z(block):
    n = lax.axis_size("z")
    here = lax.axis_index("z")
    tokens, feats = block.shape
    half = tokens // 2
    out = jnp.zeros((tokens, n * feats), block.dtype)

    def put(out, piece, part, source):
        return lax.dynamic_update_slice(out, piece, (part * half, (source % n) * feats))

    out = lax.dynamic_update_slice(out, block, (0, here * feats))
    pieces = [block[:half], block[half:]]
    right, left = list(pieces), list(pieces)
    for hop in range(1, n // 2 + 1):
        last = hop == n // 2
        for part in range(2):
            if not last or part == 0:
                right[part] = lax.ppermute(right[part], "z", shift(n, 1))
            if not last or part == 1:
                left[part] = lax.ppermute(left[part], "z", shift(n, -1))
        for part in range(2):
            if not last or part == 0:
                out = put(out, right[part], part, here - hop + n)
            if not last or part == 1:
                out = put(out, left[part], part, here + hop)
    return out


def gather_ctx(item):
    core, y = lax.axis_index("core"), lax.axis_index("y")
    n = lax.axis_size("y")
    other = lax.ppermute(item, "core", [(0, 1), (1, 0)])
    pair = jnp.where(core == 0, jnp.stack([item, other]), jnp.stack([other, item]))
    parts = [pair] + [lax.ppermute(pair, "y", shift(n, i)) for i in range(1, n)]
    out = jnp.zeros((n,) + pair.shape, item.dtype)
    for i, part in enumerate(parts):
        out = lax.dynamic_update_slice(out, part[None], ((y - i + n) % n, 0, 0, 0))
    return out.reshape((2 * n,) + item.shape)


def local(query, key, value, out_grad, out_weight, rate, residue):
    tokens, channels = query.shape
    groups, poles = rate.shape
    feats = out_weight.shape[0]
    y, core, x = lax.axis_index("y"), lax.axis_index("core"), lax.axis_index("x")
    nx = lax.axis_size("x")
    mine = (y * 2 + core).astype(jnp.int32).reshape(1)
    swap = [(0, 1), (1, 0)]
    every = groups * poles

    rate_col = jnp.broadcast_to(rate.reshape(every, 1), (every, BLK))
    res_col = jnp.broadcast_to(residue.reshape(every, 1), (every, BLK))
    rate_two = jnp.pad(jnp.concatenate([rate, rate], axis=1), ((0, 0), (0, BLK - 2 * poles)))
    rate_row, res_row = rate.reshape(1, every), residue.reshape(1, every)
    rate_nc = jnp.repeat(rate.T, channels // groups, axis=1)

    grads = gather_z(out_grad)

    rows_x = feats // nx
    half_rows = rows_x // 2
    weights = [lax.dynamic_slice(out_weight, (x * rows_x, 0), (rows_x, channels))]
    for i in range(1, nx):
        to = (x + i) % nx
        piece = lax.dynamic_slice(
            out_weight, (to * rows_x + core * half_rows, 0), (half_rows, channels)
        )
        got = lax.ppermute(piece, "x", shift(nx, i))
        other = lax.ppermute(got, "core", swap)
        weights.append(
            jnp.where(
                core == 0,
                jnp.concatenate([got, other], axis=0),
                jnp.concatenate([other, got], axis=0),
            )
        )

    sds = jax.ShapeDtypeStruct
    conv_own, ends, xt, states = call(
        forward_kernel,
        [
            sds((tokens, channels), F32),
            sds((2 * poles, channels), F32),
            sds((channels, tokens), BF16),
            sds((groups, tokens // BLK * (channels // groups), BLK), F32),
        ],
        [
            pltpu.VMEM((channels, tokens), F32),
            pltpu.VMEM((groups, tokens // BLK * (channels // groups), 2 * BLK), F32),
            pltpu.VMEM((channels, BLK), F32),
        ],
        [key, value, rate_col, res_col, rate_two],
    )
    all_ends = gather_ctx(ends)
    conv, gated, entering = call(
        enter_kernel,
        [
            sds((tokens, channels), F32),
            sds((tokens, channels), BF16),
            sds((2 * poles, channels), F32),
        ],
        [],
        [mine, all_ends, conv_own, query, rate_row, res_row, rate_nc],
        scalars=1,
    )

    partial = [
        jnp.dot(grads, weights[i], preferred_element_type=F32).astype(BF16) for i in (2, 1, 3, 0)
    ]
    two, one, three, own = partial
    got = [
        lax.ppermute(part, "x", shift(nx, -i)) for i, part in ((2, two), (1, one), (3, three))
    ]

    gates = [gated] + [lax.ppermute(gated, "x", shift(nx, i)) for i in range(1, nx)]

    d_query, back_own, pay = call(
        backward_kernel,
        [
            sds((tokens, channels), BF16),
            sds((tokens, channels), F32),
            sds((3 * poles, channels), F32),
        ],
        [
            pltpu.VMEM((channels, tokens), BF16),
            pltpu.VMEM((channels, tokens), F32),
            pltpu.VMEM((groups, tokens // BLK * (channels // groups), 2 * BLK), F32),
            pltpu.VMEM((groups, tokens // BLK * (channels // groups), BLK), F32),
            pltpu.VMEM((channels, BLK), F32),
            pltpu.VMEM((2, channels, BLK), F32),
        ],
        [own] + got + [query, conv, xt, states, entering, rate_col, res_col, rate_two, rate_nc],
    )
    all_pay = gather_ctx(pay)
    d_key, d_value, d_residue, d_rate = call(
        leave_kernel,
        [
            sds((tokens, channels), BF16),
            sds((tokens, channels), BF16),
            sds((groups, poles), F32),
            sds((groups, poles), F32),
        ],
        [],
        [mine, all_pay, back_own, key, value, rate_row, res_row, rate_nc, residue],
        scalars=1,
    )

    gate_all = jnp.stack(gates)
    mine_e = lax.dynamic_slice(grads, (0, core * half_rows), (tokens, half_rows))
    other_e = lax.dynamic_slice(grads, (0, (1 - core) * half_rows), (tokens, half_rows))
    away = jnp.einsum("te,itc->iec", other_e, gate_all, preferred_element_type=F32).astype(BF16)
    came = lax.ppermute(away, "core", swap)
    here = jnp.einsum("te,itc->iec", mine_e, gate_all, preferred_element_type=F32)
    chip = (here + came.astype(F32)).astype(BF16)
    pieces = []
    for r in range(nx):
        piece = lax.dynamic_index_in_dim(chip, (x - y - r + 2 * nx) % nx, 0, keepdims=False)
        route = [
            (a * nx + b, b * nx + (a + r) % nx) for a in range(nx) for b in range(nx)
        ]
        pieces.append(lax.ppermute(piece, ("y", "x"), route))
    total = sum(piece.astype(F32) for piece in pieces)
    d_weight = total * (1.0 / float(tokens * 2 * nx))
    return (d_query, d_key, d_value, d_weight, d_residue, d_rate)


def solution(mesh):
    fine = Mesh(mesh.devices.reshape(4, 2, 4, 8), ("y", "core", "x", "z"))
    both = P(CTX, CHAN)
    param = P(CHAN, None)
    return jax.shard_map(
        local,
        mesh=fine,
        in_specs=(both, both, both, both, P(None, CHAN), param, param),
        out_specs=(both, both, both, both, param, param),
        check_vma=False,
    )
```

```python
import functools

import jax
import jax.numpy as jnp
from jax import lax
from jax.experimental import pallas as pl
from jax.experimental.pallas import tpu as pltpu
from jax.sharding import Mesh
from jax.sharding import PartitionSpec as P

BLK = 128
TILE = 256
F32 = jnp.float32
BF16 = jnp.bfloat16
VMEM_LIMIT = 56 * 1024 * 1024
CTX = ("y", "core")
CHAN = ("x", "z")


def split(x):
    hi = x.astype(BF16)
    return hi, (x - hi.astype(F32)).astype(BF16)


def mm(a, b, ca=1, cb=0):
    return lax.dot_general(a, b, (((ca,), (cb,)), ((), ())), preferred_element_type=F32)


def lanes(shape):
    return lax.broadcasted_iota(jnp.int32, shape, 1).astype(F32)


def rows(shape):
    return lax.broadcasted_iota(jnp.int32, shape, 0).astype(F32)


def exact(a, b, ca, cb):
    return lax.dot_general(
        a, b, (((ca,), (cb,)), ((), ())), preferred_element_type=F32, precision=lax.Precision.HIGHEST
    )


def by_column(param):
    turned = param.T
    groups, poles = param.shape
    return jnp.concatenate(
        [jnp.broadcast_to(turned[:, g : g + 1], (poles, BLK)) for g in range(groups)], axis=0
    )


def by_lane(param):
    groups, poles = param.shape
    return jnp.concatenate([param, param, jnp.zeros((groups, BLK - 2 * poles), F32)], axis=1)


def indicator(groups, channels):
    shape = (groups, channels)
    return (
        lax.broadcasted_iota(jnp.int32, shape, 0)
        == lax.broadcasted_iota(jnp.int32, shape, 1) // (channels // groups)
    ).astype(F32)


def by_channel(param, channels):
    return exact(param, indicator(param.shape[0], channels), 0, 0)


def stacked(ref, g, width, blocks):
    return jnp.concatenate(
        [ref[g * width : (g + 1) * width, b * BLK : (b + 1) * BLK] for b in range(blocks)], axis=0
    )


def with_states(x, taps, state, lead_hi, lead_lo):
    poles = lead_hi.shape[0]
    none = jnp.zeros((BLK - poles, BLK), BF16)
    s_hi, s_lo = split(state)
    first = mm(
        jnp.concatenate([x, s_hi], axis=1), jnp.concatenate([taps, lead_hi, none], axis=0)
    )
    second = mm(
        jnp.concatenate([s_lo, s_hi], axis=1),
        jnp.concatenate([lead_hi, none, lead_lo, none], axis=0),
    )
    return first + second


def sums_rhs(top, second, third, fourth):
    poles = top[0].shape[0]
    none = jnp.zeros((poles, 2 * BLK), BF16)
    rest = jnp.zeros((BLK - 2 * poles, 2 * BLK), BF16)

    def part(pair):
        return none if pair is None else jnp.concatenate(pair, axis=1)

    return jnp.concatenate(
        [part(top), part(second), rest, part(third), part(fourth), rest], axis=0
    )


def forward_kernel(
    key_ref, value_ref, rate_ref, res_ref, conv_ref, ends_ref, xt_ref, states_ref, ct_ref, sums_ref, fin_ref
):
    tokens, channels = key_ref.shape
    groups, poles = rate_ref.shape
    width, blocks = channels // groups, tokens // BLK
    for b in range(blocks):
        at = slice(b * BLK, (b + 1) * BLK)
        inner = key_ref[at, :].astype(F32) * value_ref[at, :].astype(F32)
        xt_ref[:, at] = inner.T.astype(BF16)
    rate, res = by_column(rate_ref[...]), by_column(res_ref[...])
    time = lanes(rate.shape)
    u_hi, u_lo = split(res * jnp.exp(-rate * (time - 64.0)))
    v_hi, v_lo = split(jnp.exp(rate * (time - 64.0)))
    tail_all = jnp.exp(-rate * (BLK - 1.0 - time))
    tail = split(tail_all)
    tail_lag = split((BLK - 1.0 - time) * tail_all)
    lead = split(res * jnp.exp(-rate * (time + 1.0)))
    for g in range(groups):
        own = slice(g * poles, (g + 1) * poles)
        x = stacked(xt_ref, g, width, blocks)
        top = tuple(part[own] for part in tail)
        lag = tuple(part[own] for part in tail_lag)
        sums_ref[g] = mm(
            jnp.concatenate([x, x], axis=1), sums_rhs(top, lag, None, top), 1, 1
        )
    rate_two = by_lane(rate_ref[...])
    span = jnp.exp(-float(BLK) * rate_two)
    lane = lanes((1, BLK))
    for g in range(groups):
        step = span[g : g + 1, :]
        couple = jnp.where(lane >= poles, float(BLK) * step, 0.0)
        state = jnp.zeros((width, BLK), F32)
        twin = jnp.zeros((width, BLK), F32)
        for b in range(blocks):
            at = slice(b * width, (b + 1) * width)
            states_ref[g, at, :] = state
            state = step * state + couple * twin + sums_ref[g, at, :BLK]
            twin = step * twin + sums_ref[g, at, BLK:]
        fin_ref[g * width : (g + 1) * width, :] = state
    ends_ref[...] = fin_ref[...].T[: 2 * poles, :]
    causal = lanes((BLK, BLK)) >= rows((BLK, BLK))
    for g in range(groups):
        own = slice(g * poles, (g + 1) * poles)
        x = stacked(xt_ref, g, width, blocks)
        taps = mm(
            jnp.concatenate([v_hi[own], v_lo[own], v_hi[own]], axis=0),
            jnp.concatenate([u_hi[own], u_hi[own], u_lo[own]], axis=0),
            0,
            0,
        )
        taps = jnp.where(causal, taps, 0.0).astype(BF16)
        out = with_states(x, taps, states_ref[g], lead[0][own], lead[1][own])
        for b in range(blocks):
            ct_ref[g * width : (g + 1) * width, b * BLK : (b + 1) * BLK] = out[
                b * width : (b + 1) * width
            ]
    for b in range(blocks):
        at = slice(b * BLK, (b + 1) * BLK)
        conv_ref[at, :] = ct_ref[:, at].T


def spread(state, groups):
    poles, channels = state.shape
    width = channels // groups
    tall = jnp.concatenate([state] * groups, axis=0)
    row = lax.broadcasted_iota(jnp.int32, tall.shape, 0) // poles
    col = lax.broadcasted_iota(jnp.int32, tall.shape, 1) // width
    return jnp.where(row == col, tall, 0.0)


def modes(lead, state_tall):
    l_hi, l_lo = split(lead)
    s_hi, s_lo = split(state_tall)
    return mm(l_hi, s_hi) + mm(l_hi, s_lo) + mm(l_lo, s_hi)


def enter_kernel(
    here_ref, all_ref, conv_ref, query_ref, rate_ref, res_ref, conv_out_ref, gated_ref, in_ref
):
    tokens, channels = conv_ref.shape
    groups, poles = rate_ref.shape
    mine = 2 * here_ref[0] + here_ref[1]
    count = all_ref.shape[0]
    rate_nc = by_channel(rate_ref[...], channels)
    rate_row, res_row = by_column(rate_ref[...]).T, by_column(res_ref[...]).T
    state = jnp.zeros((poles, channels), F32)
    slope = jnp.zeros((poles, channels), F32)
    for place in range(count):
        gap = (mine - 1 - place).astype(F32)
        lag = jnp.maximum(gap, 0.0) * float(tokens)
        weight = jnp.where(gap >= 0.0, jnp.exp(-rate_nc * lag), 0.0)
        end = all_ref[place, :poles, :]
        state = state + weight * end
        slope = slope + weight * (all_ref[place, poles:, :] + lag * end)
    in_ref[:poles, :] = state
    in_ref[poles:, :] = slope
    tall = spread(state, groups)
    for b in range(tokens // BLK):
        at = slice(b * BLK, (b + 1) * BLK)
        time = rows((BLK, groups * poles)) + float(b * BLK + 1)
        lead = res_row * jnp.exp(-rate_row * time)
        conv = conv_ref[at, :] + modes(lead, tall)
        conv_out_ref[at, :] = conv
        gated_ref[:, at] = (query_ref[at, :].astype(F32) * conv).T.astype(BF16)


def backward_kernel(
    own_ref, p1_ref, p2_ref, p3_ref, query_ref, conv_ref, xt_ref, states_ref, in_ref, rate_ref, res_ref,
    dq_ref, back_ref, pay_ref, gt_ref, bt_ref, sums_ref, rs_ref, fin_ref, cross_ref
):
    tokens, channels = query_ref.shape
    groups, poles = rate_ref.shape
    width, blocks = channels // groups, tokens // BLK
    for b in range(blocks):
        at = slice(b * BLK, (b + 1) * BLK)
        total = (own_ref[at, :].astype(F32) + p1_ref[at, :].astype(F32)) + (
            p2_ref[at, :].astype(F32) + p3_ref[at, :].astype(F32)
        )
        grad = total.astype(BF16).astype(F32)
        dq_ref[at, :] = (grad * conv_ref[at, :]).astype(BF16)
        gt_ref[:, at] = (grad * query_ref[at, :].astype(F32)).T.astype(BF16)
    rate, res = by_column(rate_ref[...]), by_column(res_ref[...])
    time = lanes(rate.shape)
    u_hi, u_lo = split(res * jnp.exp(-rate * (time - 64.0)))
    v_all = jnp.exp(rate * (time - 64.0))
    v_hi, v_lo = split(v_all)
    w_hi, w_lo = split((time - 64.0) * v_all)
    head_all = jnp.exp(-rate * time)
    head = split(head_all)
    head_lag = split(time * head_all)
    trail = split(res * jnp.exp(-rate * (BLK - time)))
    for g in range(groups):
        own = slice(g * poles, (g + 1) * poles)
        y = stacked(gt_ref, g, width, blocks)
        top = tuple(part[own] for part in head)
        lag = tuple(part[own] for part in head_lag)
        sums_ref[g] = mm(jnp.concatenate([y, y], axis=1), sums_rhs(top, lag, lag, top), 1, 1)
    rate_two = by_lane(rate_ref[...])
    span = jnp.exp(-float(BLK) * rate_two)
    lane = lanes((1, BLK))
    low = lane < poles
    for g in range(groups):
        step = span[g : g + 1, :]
        couple = jnp.where(lane >= poles, float(BLK) * step, 0.0)
        state = jnp.zeros((width, BLK), F32)
        twin = jnp.zeros((width, BLK), F32)
        res_sum = jnp.zeros((width, BLK), F32)
        rate_sum = jnp.zeros((width, BLK), F32)
        for b in reversed(range(blocks)):
            at = slice(b * width, (b + 1) * width)
            rs_ref[g, at, :] = state
            first, second = sums_ref[g, at, :BLK], sums_ref[g, at, BLK:]
            before = states_ref[g, at, :]
            res_sum = res_sum + jnp.where(low, first * before, 0.0)
            rate_sum = rate_sum + (second + jnp.where(low, first, 0.0)) * before
            state, twin = (
                step * state + couple * twin + first,
                step * twin + jnp.where(low, 0.0, second),
            )
        fin_ref[g * width : (g + 1) * width, :] = state
        decay = jnp.exp(-rate_two[g : g + 1, :])
        cross_ref[0, g * width : (g + 1) * width, :] = decay * res_sum
        cross_ref[1, g * width : (g + 1) * width, :] = decay * rate_sum
    causal = rows((BLK, BLK)) >= lanes((BLK, BLK))
    for g in range(groups):
        own = slice(g * poles, (g + 1) * poles)
        y = stacked(gt_ref, g, width, blocks)
        taps = mm(
            jnp.concatenate([u_hi[own], u_hi[own], u_lo[own]], axis=0),
            jnp.concatenate([v_hi[own], v_lo[own], v_hi[own]], axis=0),
            0,
            0,
        )
        taps = jnp.where(causal, taps, 0.0).astype(BF16)
        out = with_states(y, taps, rs_ref[g], trail[0][own], trail[1][own])
        for b in range(blocks):
            bt_ref[g * width : (g + 1) * width, b * BLK : (b + 1) * BLK] = out[
                b * width : (b + 1) * width
            ]
        x = stacked(xt_ref, g, width, blocks)
        pairs = jnp.where(causal, mm(y, x, 0, 0), 0.0).astype(BF16)
        rhs = jnp.concatenate(
            [
                jnp.concatenate([v_hi[own], v_lo[own]], axis=1),
                jnp.concatenate([w_hi[own], w_lo[own]], axis=1),
                jnp.zeros((BLK - 2 * poles, 2 * BLK), BF16),
            ],
            axis=0,
        )
        held = mm(jnp.concatenate([pairs, pairs], axis=1), rhs, 1, 1)
        since = rows((BLK, BLK)) - 64.0
        held = held * jnp.exp(-rate_two[g : g + 1, :] * since)
        res_row = jnp.sum(jnp.where(low, held, 0.0), axis=0, keepdims=True)
        rate_row = jnp.sum(jnp.where(low, since * held, -held), axis=0, keepdims=True)
        one = slice(g * width, g * width + 1)
        cross_ref[0, one, :] = cross_ref[0, one, :] + res_row
        cross_ref[1, one, :] = cross_ref[1, one, :] + rate_row
    starts = fin_ref[...].T
    start, start_lag = starts[:poles], starts[poles : 2 * poles]
    state_in, slope_in = in_ref[:poles, :], in_ref[poles:, :]
    decay = jnp.exp(-by_channel(rate_ref[...], channels))
    res_cross = cross_ref[0].T[:poles]
    rate_cross = cross_ref[1].T
    pay_ref[:poles, :] = start
    pay_ref[poles : 2 * poles, :] = res_cross + decay * start * state_in
    pay_ref[2 * poles :, :] = (
        rate_cross[:poles]
        + rate_cross[poles : 2 * poles]
        + decay * ((start_lag + start) * state_in + start * slope_in)
    )
    for b in range(blocks):
        at = slice(b * BLK, (b + 1) * BLK)
        back_ref[at, :] = bt_ref[:, at].T


def leave_kernel(
    here_ref, all_ref, back_ref, key_ref, value_ref, rate_ref, res_ref, dk_ref, dv_ref, dres_ref, drate_ref
):
    tokens, channels = back_ref.shape
    groups, poles = rate_ref.shape
    mine = 2 * here_ref[0] + here_ref[1]
    count = all_ref.shape[0]
    rate_nc = by_channel(rate_ref[...], channels)
    rate_row, res_row = by_column(rate_ref[...]).T, by_column(res_ref[...]).T
    state = jnp.zeros((poles, channels), F32)
    total = jnp.zeros((2 * poles, channels), F32)
    for place in range(count):
        gap = (place - 1 - mine).astype(F32)
        lag = jnp.maximum(gap, 0.0) * float(tokens)
        weight = jnp.where(gap >= 0.0, jnp.exp(-rate_nc * lag), 0.0)
        state = state + weight * all_ref[place, :poles, :]
        total = total + all_ref[place, poles:, :]
    tall = spread(state, groups)
    scale = 1.0 / float(tokens * count)
    both = exact(indicator(groups, channels), total, 1, 1)
    dres_ref[...] = both[:, :poles] * scale
    drate_ref[...] = -res_ref[...] * both[:, poles:] * scale
    for b in range(tokens // BLK):
        at = slice(b * BLK, (b + 1) * BLK)
        time = float(tokens - b * BLK) - rows((BLK, groups * poles))
        trail = res_row * jnp.exp(-rate_row * time)
        back = back_ref[at, :] + modes(trail, tall)
        dk_ref[at, :] = (back * value_ref[at, :].astype(F32)).astype(BF16)
        dv_ref[at, :] = (back * key_ref[at, :].astype(F32)).astype(BF16)


def block_copies(z, refs, to_ref, sem):
    own, r1, l1, r2, l2, r3, l3, r4, l4 = refs
    half = r4.shape[0]
    whole = ((0, own), (-1, r1), (1, l1), (-2, r2), (2, l2), (-3, r3), (3, l3))
    nz = len(whole) + 1
    for far, ref in whole:
        at = lax.rem(z + far + nz, nz)
        yield at, ref, lambda slot: to_ref.at[slot], lambda slot: sem.at[slot, 0]
    at = lax.rem(z + nz // 2, nz)
    yield at, r4, lambda slot: to_ref.at[slot, pl.ds(0, half), :], lambda slot: sem.at[slot, 0]
    yield at, l4, lambda slot: to_ref.at[slot, pl.ds(half, half), :], lambda slot: sem.at[slot, 1]


def fetch_half(z, which, refs, half_ref, sem):
    count = half_ref.shape[0]
    far_slot = lax.rem(z + count, count)
    far_here = lax.div(lax.rem(z + count, 2 * count), count) == which
    for at, ref, place, signal in block_copies(z, refs, half_ref, sem):
        slot = lax.rem(at, count)

        @pl.when(lax.div(at, count) == which)
        def _():
            pltpu.make_async_copy(ref, place(slot), signal(slot)).start()

    def wait(j):
        split_here = jnp.logical_and(far_here, far_slot == j)
        tokens = half_ref.shape[1]

        @pl.when(split_here)
        def _():
            for part in range(2):
                piece = half_ref.at[j, pl.ds(part * (tokens // 2), tokens // 2), :]
                pltpu.make_async_copy(piece, piece, sem.at[j, part]).wait()

        @pl.when(jnp.logical_not(split_here))
        def _():
            pltpu.make_async_copy(half_ref.at[j], half_ref.at[j], sem.at[j, 0]).wait()

    return wait


def away_kernel(here_ref, *refs):
    blocks, gates, (away_ref, half_ref, sem) = refs[:9], refs[9:13], refs[13:]
    count, _, width = half_ref.shape
    wait = fetch_half(here_ref[2], 1 - here_ref[1], blocks, half_ref, sem)
    for j in range(count):
        wait(j)
        at = slice(j * width, (j + 1) * width)
        for i, gate in enumerate(gates):
            away_ref[i, :, at] = mm(gate[...], half_ref[j]).astype(BF16)


def project_kernel(here_ref, *refs):
    blocks, weight_ref, fetched, others = refs[:9], refs[9], refs[10:14], refs[14:18]
    p0_ref, p1_ref, p2_ref, p3_ref, f_ref, w_ref, f_sem, w_sem = refs[18:]
    core, z, x = here_ref[1], here_ref[2], here_ref[3]
    nz, tokens, _ = f_ref.shape
    rows_x = w_ref.shape[1]
    half = rows_x // 2
    feat = [
        pltpu.make_async_copy(ref, place(at), signal(at))
        for at, ref, place, signal in block_copies(z, blocks, f_ref, f_sem)
    ]
    weight = {
        0: [
            pltpu.make_async_copy(
                weight_ref.at[pl.ds(pl.multiple_of(x * rows_x, rows_x), rows_x), :], w_ref.at[0], w_sem.at[0]
            )
        ]
    }
    for k, (i, first) in enumerate(((1, 0), (2, 0), (2, half // 2), (3, 0))):
        for j, (ref, base) in enumerate(((fetched[k], core * half), (others[k], (1 - core) * half))):
            size = ref.shape[0]
            place = pl.ds(pl.multiple_of(base + first, half // 2), size)
            weight.setdefault(i, []).append(
                pltpu.make_async_copy(ref, w_ref.at[i, place, :], w_sem.at[2 * k + j + 1])
            )
    for copy in weight[2] + feat + weight[1] + weight[3] + weight[0]:
        copy.start()
    for copy in feat:
        copy.wait()
    tile = TILE
    for i, out in ((2, p2_ref), (1, p1_ref), (3, p3_ref), (0, p0_ref)):
        for copy in weight[i]:
            copy.wait()
        for m in range(tokens // tile):
            at = slice(m * tile, (m + 1) * tile)
            lhs = jnp.concatenate([f_ref[j, at, :] for j in range(nz)], axis=1)
            out[at, :] = mm(lhs, w_ref[i]).astype(BF16)


def chip_kernel(here_ref, *refs):
    blocks, came_ref, gates, outs, (gate_ref, half_ref, sem) = refs[:9], refs[9], refs[10:14], refs[14:18], refs[18:]
    y, core = here_ref[0], here_ref[1]
    count, _, width = half_ref.shape
    wait = fetch_half(here_ref[2], core, blocks, half_ref, sem)
    for i, gate in enumerate(gates):
        gate_ref[i] = gate[...]
    for j in range(count):
        wait(j)
        at = slice(j * width, (j + 1) * width)
        for r, out in enumerate(outs):
            i = lax.rem(8 - y - r, 4)
            part = mm(gate_ref[i], half_ref[j])
            out[:, at] = (part + came_ref[i, :, at].astype(F32)).astype(BF16)


def column_kernel(a_ref, b_ref, c_ref, d_ref, out_ref):
    total = (a_ref[...].astype(F32) + b_ref[...].astype(F32)) + (
        c_ref[...].astype(F32) + d_ref[...].astype(F32)
    )
    out_ref[...] = total.astype(BF16)


def total_kernel(scale, in_ref, out_ref):
    for b in range(in_ref.shape[1] // BLK):
        at = slice(b * BLK, (b + 1) * BLK)
        out_ref[at, :] = in_ref[:, at].astype(F32).T * scale


MIB = 2**20


def call(kernel, outs, scratch, ops, vmem, us, scalars=0, far=()):
    spec = pl.BlockSpec(memory_space=pltpu.VMEM)
    return pl.pallas_call(
        kernel,
        out_shape=outs,
        in_specs=[
            pl.BlockSpec(memory_space=pltpu.SMEM)
            if i < scalars
            else (pl.BlockSpec(memory_space=pltpu.HBM) if i in far else spec)
            for i in range(len(ops))
        ],
        out_specs=[spec] * len(outs),
        scratch_shapes=scratch,
        compiler_params=pltpu.CompilerParams(vmem_limit_bytes=vmem * MIB),
        cost_estimate=pl.CostEstimate(
            flops=1000, bytes_accessed=int(us * 3.69e6), transcendentals=0
        ),
    )(*ops)


def shift(n, by):
    return [(i, (i + by) % n) for i in range(n)]


def gather_ctx(item):
    n = lax.axis_size(CTX)
    return lax.all_to_all(
        jnp.broadcast_to(item[None], (n,) + item.shape), CTX, split_axis=0, concat_axis=0
    )


def after(value, *others):
    return lax.optimization_barrier((value, others))[0]


def local(query, key, value, out_grad, out_weight, rate, residue):
    tokens, channels = query.shape
    groups, poles = rate.shape
    feats = out_weight.shape[0]
    y, core = lax.axis_index("y"), lax.axis_index("core")
    x, z = lax.axis_index("x"), lax.axis_index("z")
    nx, ny, nz = lax.axis_size("x"), lax.axis_size("y"), lax.axis_size("z")
    here = jnp.stack([y, core, z, x]).astype(jnp.int32)
    swap = [(0, 1), (1, 0)]
    sds = jax.ShapeDtypeStruct
    half_scratch = [
        pltpu.VMEM((nz // 2, tokens, channels), BF16),
        pltpu.SemaphoreType.DMA((nz // 2, 2)),
    ]
    stack_shape = (groups, tokens // BLK * (channels // groups))

    def both_ways(axis, pair):
        n = lax.axis_size(axis)
        return (
            lax.ppermute(pair[0], axis, shift(n, 1)),
            lax.ppermute(pair[1], axis, shift(n, -1)),
        )

    rows_x = feats // nx
    half_rows = rows_x // 2

    def rows_for(by, start, size):
        first = ((x + by) % nx) * rows_x + core * half_rows + start
        return lax.dynamic_slice(out_weight, (first, 0), (size, channels))

    hop1 = both_ways("z", (out_grad, out_grad))
    near = both_ways("x", (rows_for(1, 0, half_rows), rows_for(-1, 0, half_rows)))

    conv_own, ends, xt, states = call(
        forward_kernel,
        [
            sds((tokens, channels), F32),
            sds((2 * poles, channels), F32),
            sds((channels, tokens), BF16),
            sds(stack_shape + (BLK,), F32),
        ],
        [
            pltpu.VMEM((channels, tokens), F32),
            pltpu.VMEM(stack_shape + (2 * BLK,), F32),
            pltpu.VMEM((channels, BLK), F32),
        ],
        [key, value, rate, residue],
        12,
        10.0,
    )
    hop2 = both_ways("z", after(hop1, near, ends))
    half_a = both_ways("x", (rows_for(2, 0, half_rows // 2), rows_for(2, half_rows // 2, half_rows // 2)))
    all_ends = gather_ctx(ends)
    conv, gated, entering = call(
        enter_kernel,
        [
            sds((tokens, channels), F32),
            sds((channels, tokens), BF16),
            sds((2 * poles, channels), F32),
        ],
        [],
        [here, all_ends, conv_own, query, rate, residue],
        8,
        10.0,
        scalars=1,
    )
    hop3 = both_ways("z", after(hop2, gated, half_a))
    half_b = both_ways("x", half_a)
    sent = after(gated, half_b)
    gates = [gated] + [lax.ppermute(sent, "x", shift(nx, i)) for i in range(1, nx)]
    fetched = [near[0], *half_b, near[1]]
    others = [lax.ppermute(piece, "core", swap) for piece in fetched]
    right, left = after(hop3, others)
    hop4 = both_ways("z", (right[: tokens // 2], left[tokens // 2 :]))
    blocks = [out_grad, *hop1, *hop2, *hop3, *hop4]

    own, one, two, three = call(
        project_kernel,
        [sds((tokens, channels), BF16)] * nx,
        [
            pltpu.VMEM((nz, tokens, channels), BF16),
            pltpu.VMEM((nx, rows_x, channels), BF16),
            pltpu.SemaphoreType.DMA((nz, 2)),
            pltpu.SemaphoreType.DMA((2 * nx + 1,)),
        ],
        [here] + blocks + [out_weight] + fetched + others,
        16,
        6.0,
        scalars=1,
        far=tuple(range(1, 19)),
    )
    sums = [
        lax.ppermute(part, "x", shift(nx, -i)) for i, part in ((2, two), (1, one), (3, three))
    ]

    (away,) = call(
        away_kernel,
        [sds((nx, channels, half_rows), BF16)],
        half_scratch,
        [here] + after(blocks, own) + gates,
        12,
        0.5,
        scalars=1,
        far=tuple(range(1, 10)),
    )
    came = lax.ppermute(away, "core", swap)

    chip = call(
        chip_kernel,
        [sds((channels, half_rows), BF16)] * nx,
        [pltpu.VMEM((nx, channels, tokens), BF16)] + half_scratch,
        [here] + blocks + [came] + gates,
        16,
        0.5,
        scalars=1,
        far=tuple(range(1, 10)),
    )
    parts = [chip[0]] + [lax.ppermute(chip[r], "y", shift(ny, r)) for r in range(1, ny)]
    d_query, back_own, pay = call(
        backward_kernel,
        [
            sds((tokens, channels), BF16),
            sds((tokens, channels), F32),
            sds((3 * poles, channels), F32),
        ],
        [
            pltpu.VMEM((channels, tokens), BF16),
            pltpu.VMEM((channels, tokens), F32),
            pltpu.VMEM(stack_shape + (2 * BLK,), F32),
            pltpu.VMEM(stack_shape + (BLK,), F32),
            pltpu.VMEM((channels, BLK), F32),
            pltpu.VMEM((2, channels, BLK), F32),
        ],
        [after(own, chip)] + sums + [query, conv, xt, states, entering, rate, residue],
        16,
        20.0,
    )
    parts[0] = after(parts[0], pay)
    (column,) = call(column_kernel, [sds((channels, half_rows), BF16)], [], parts, 8, 1.0)
    all_pay = gather_ctx(after(pay, column))
    route = [(a * nx + b, b * nx + (a + b) % nx) for a in range(ny) for b in range(nx)]
    column = lax.ppermute(column, ("y", "x"), route)

    d_key, d_value, d_residue, d_rate = call(
        leave_kernel,
        [
            sds((tokens, channels), BF16),
            sds((tokens, channels), BF16),
            sds((groups, poles), F32),
            sds((groups, poles), F32),
        ],
        [],
        [here, all_pay, back_own, key, value, rate, residue],
        8,
        2.5,
        scalars=1,
    )
    (d_weight,) = call(
        functools.partial(total_kernel, 1.0 / float(tokens * 2 * nx)),
        [sds((half_rows, channels), F32)],
        [],
        [column],
        8,
        1.5,
    )
    return (d_query, d_key, d_value, d_weight, d_residue, d_rate)


def solution(mesh):
    fine = Mesh(mesh.devices.reshape(4, 2, 4, 8), ("y", "core", "x", "z"))
    both = P(CTX, CHAN)
    param = P(CHAN, None)
    return jax.shard_map(
        local,
        mesh=fine,
        in_specs=(both, both, both, both, P(None, CHAN), param, param),
        out_specs=(both, both, both, both, param, param),
        check_vma=False,
    )
```

```python
import functools

import jax
import jax.numpy as jnp
from jax import lax
from jax.experimental import pallas as pl
from jax.experimental.pallas import tpu as pltpu
from jax.sharding import Mesh
from jax.sharding import PartitionSpec as P

BLK = 128
TILE = 256
F32 = jnp.float32
BF16 = jnp.bfloat16
VMEM_LIMIT = 56 * 1024 * 1024
CTX = ("y", "core")
CHAN = ("x", "z")


def split(x):
    hi = x.astype(BF16)
    return hi, (x - hi.astype(F32)).astype(BF16)


def mm(a, b, ca=1, cb=0):
    return lax.dot_general(a, b, (((ca,), (cb,)), ((), ())), preferred_element_type=F32)


def lanes(shape):
    return lax.broadcasted_iota(jnp.int32, shape, 1).astype(F32)


def rows(shape):
    return lax.broadcasted_iota(jnp.int32, shape, 0).astype(F32)


def exact(a, b, ca, cb):
    return lax.dot_general(
        a, b, (((ca,), (cb,)), ((), ())), preferred_element_type=F32, precision=lax.Precision.HIGHEST
    )


def by_column(param):
    turned = param.T
    groups, poles = param.shape
    return jnp.concatenate(
        [jnp.broadcast_to(turned[:, g : g + 1], (poles, BLK)) for g in range(groups)], axis=0
    )


def by_lane(param):
    groups, poles = param.shape
    return jnp.concatenate([param, param, jnp.zeros((groups, BLK - 2 * poles), F32)], axis=1)


def indicator(groups, channels):
    shape = (groups, channels)
    return (
        lax.broadcasted_iota(jnp.int32, shape, 0)
        == lax.broadcasted_iota(jnp.int32, shape, 1) // (channels // groups)
    ).astype(F32)


def by_channel(param, channels):
    return exact(param, indicator(param.shape[0], channels), 0, 0)


def stacked(ref, g, width, blocks):
    return jnp.concatenate(
        [ref[g * width : (g + 1) * width, b * BLK : (b + 1) * BLK] for b in range(blocks)], axis=0
    )


def with_states(x, taps, state, lead_hi, lead_lo):
    poles = lead_hi.shape[0]
    none = jnp.zeros((BLK - poles, BLK), BF16)
    s_hi, s_lo = split(state)
    first = mm(
        jnp.concatenate([x, s_hi], axis=1), jnp.concatenate([taps, lead_hi, none], axis=0)
    )
    second = mm(
        jnp.concatenate([s_lo, s_hi], axis=1),
        jnp.concatenate([lead_hi, none, lead_lo, none], axis=0),
    )
    return first + second


def sums_rhs(top, second, third, fourth):
    poles = top[0].shape[0]
    none = jnp.zeros((poles, 2 * BLK), BF16)
    rest = jnp.zeros((BLK - 2 * poles, 2 * BLK), BF16)

    def part(pair):
        return none if pair is None else jnp.concatenate(pair, axis=1)

    return jnp.concatenate(
        [part(top), part(second), rest, part(third), part(fourth), rest], axis=0
    )


def forward_kernel(
    key_ref, value_ref, rate_ref, res_ref, conv_ref, ends_ref, xt_ref, states_ref, ct_ref, sums_ref, fin_ref
):
    tokens, channels = key_ref.shape
    groups, poles = rate_ref.shape
    width, blocks = channels // groups, tokens // BLK
    for b in range(blocks):
        at = slice(b * BLK, (b + 1) * BLK)
        inner = key_ref[at, :].astype(F32) * value_ref[at, :].astype(F32)
        xt_ref[:, at] = inner.T.astype(BF16)
    rate, res = by_column(rate_ref[...]), by_column(res_ref[...])
    time = lanes(rate.shape)
    u_hi, u_lo = split(res * jnp.exp(-rate * (time - 64.0)))
    v_hi, v_lo = split(jnp.exp(rate * (time - 64.0)))
    tail_all = jnp.exp(-rate * (BLK - 1.0 - time))
    tail = split(tail_all)
    tail_lag = split((BLK - 1.0 - time) * tail_all)
    lead = split(res * jnp.exp(-rate * (time + 1.0)))
    for g in range(groups):
        own = slice(g * poles, (g + 1) * poles)
        x = stacked(xt_ref, g, width, blocks)
        top = tuple(part[own] for part in tail)
        lag = tuple(part[own] for part in tail_lag)
        sums_ref[g] = mm(
            jnp.concatenate([x, x], axis=1), sums_rhs(top, lag, None, top), 1, 1
        )
    rate_two = by_lane(rate_ref[...])
    span = jnp.exp(-float(BLK) * rate_two)
    lane = lanes((1, BLK))
    for g in range(groups):
        step = span[g : g + 1, :]
        couple = jnp.where(lane >= poles, float(BLK) * step, 0.0)
        state = jnp.zeros((width, BLK), F32)
        twin = jnp.zeros((width, BLK), F32)
        for b in range(blocks):
            at = slice(b * width, (b + 1) * width)
            states_ref[g, at, :] = state
            state = step * state + couple * twin + sums_ref[g, at, :BLK]
            twin = step * twin + sums_ref[g, at, BLK:]
        fin_ref[g * width : (g + 1) * width, :] = state
    ends_ref[...] = fin_ref[...].T[: 2 * poles, :]
    causal = lanes((BLK, BLK)) >= rows((BLK, BLK))
    for g in range(groups):
        own = slice(g * poles, (g + 1) * poles)
        x = stacked(xt_ref, g, width, blocks)
        taps = mm(
            jnp.concatenate([v_hi[own], v_lo[own], v_hi[own]], axis=0),
            jnp.concatenate([u_hi[own], u_hi[own], u_lo[own]], axis=0),
            0,
            0,
        )
        taps = jnp.where(causal, taps, 0.0).astype(BF16)
        out = with_states(x, taps, states_ref[g], lead[0][own], lead[1][own])
        for b in range(blocks):
            ct_ref[g * width : (g + 1) * width, b * BLK : (b + 1) * BLK] = out[
                b * width : (b + 1) * width
            ]
    for b in range(blocks):
        at = slice(b * BLK, (b + 1) * BLK)
        conv_ref[at, :] = ct_ref[:, at].T


def spread(state, groups):
    poles, channels = state.shape
    width = channels // groups
    tall = jnp.concatenate([state] * groups, axis=0)
    row = lax.broadcasted_iota(jnp.int32, tall.shape, 0) // poles
    col = lax.broadcasted_iota(jnp.int32, tall.shape, 1) // width
    return jnp.where(row == col, tall, 0.0)


def modes(lead, state_tall):
    l_hi, l_lo = split(lead)
    s_hi, s_lo = split(state_tall)
    return mm(l_hi, s_hi) + mm(l_hi, s_lo) + mm(l_lo, s_hi)


def arrived(y, core, own_ref, other_ref, pair_refs):
    count = len(pair_refs) + 1
    yield 2 * y + core, lambda lo, hi: own_ref[lo:hi, :]
    yield 2 * y + 1 - core, lambda lo, hi: other_ref[lo:hi, :]
    for i, ref in enumerate(pair_refs, 1):
        far = lax.rem(y - i + count, count)
        yield 2 * far + core, lambda lo, hi, ref=ref: ref[0, lo:hi, :]
        yield 2 * far + 1 - core, lambda lo, hi, ref=ref: ref[1, lo:hi, :]


def enter_kernel(
    here_ref, own_ref, other_ref, p1_ref, p2_ref, p3_ref, conv_ref, query_ref, rate_ref, res_ref, conv_out_ref, gated_ref, in_ref
):
    tokens, channels = conv_ref.shape
    groups, poles = rate_ref.shape
    y, core = here_ref[0], here_ref[1]
    mine = 2 * y + core
    rate_nc = by_channel(rate_ref[...], channels)
    rate_row, res_row = by_column(rate_ref[...]).T, by_column(res_ref[...]).T
    state = jnp.zeros((poles, channels), F32)
    slope = jnp.zeros((poles, channels), F32)
    for place, read in arrived(y, core, own_ref, other_ref, (p1_ref, p2_ref, p3_ref)):
        gap = (mine - 1 - place).astype(F32)
        lag = jnp.maximum(gap, 0.0) * float(tokens)
        weight = jnp.where(gap >= 0.0, jnp.exp(-rate_nc * lag), 0.0)
        end = read(0, poles)
        state = state + weight * end
        slope = slope + weight * (read(poles, 2 * poles) + lag * end)
    in_ref[:poles, :] = state
    in_ref[poles:, :] = slope
    tall = spread(state, groups)
    for b in range(tokens // BLK):
        at = slice(b * BLK, (b + 1) * BLK)
        time = rows((BLK, groups * poles)) + float(b * BLK + 1)
        lead = res_row * jnp.exp(-rate_row * time)
        conv = conv_ref[at, :] + modes(lead, tall)
        conv_out_ref[at, :] = conv
        gated_ref[:, at] = (query_ref[at, :].astype(F32) * conv).T.astype(BF16)


def backward_kernel(
    own_ref, p1_ref, p2_ref, p3_ref, query_ref, conv_ref, xt_ref, states_ref, in_ref, rate_ref, res_ref,
    dq_ref, back_ref, pay_ref, gt_ref, bt_ref, sums_ref, rs_ref, fin_ref, cross_ref
):
    tokens, channels = query_ref.shape
    groups, poles = rate_ref.shape
    width, blocks = channels // groups, tokens // BLK
    for b in range(blocks):
        at = slice(b * BLK, (b + 1) * BLK)
        total = (own_ref[at, :].astype(F32) + p1_ref[at, :].astype(F32)) + (
            p2_ref[at, :].astype(F32) + p3_ref[at, :].astype(F32)
        )
        grad = total.astype(BF16).astype(F32)
        dq_ref[at, :] = (grad * conv_ref[at, :]).astype(BF16)
        gt_ref[:, at] = (grad * query_ref[at, :].astype(F32)).T.astype(BF16)
    rate, res = by_column(rate_ref[...]), by_column(res_ref[...])
    time = lanes(rate.shape)
    u_hi, u_lo = split(res * jnp.exp(-rate * (time - 64.0)))
    v_all = jnp.exp(rate * (time - 64.0))
    v_hi, v_lo = split(v_all)
    w_hi, w_lo = split((time - 64.0) * v_all)
    head_all = jnp.exp(-rate * time)
    head = split(head_all)
    head_lag = split(time * head_all)
    trail = split(res * jnp.exp(-rate * (BLK - time)))
    for g in range(groups):
        own = slice(g * poles, (g + 1) * poles)
        y = stacked(gt_ref, g, width, blocks)
        top = tuple(part[own] for part in head)
        lag = tuple(part[own] for part in head_lag)
        sums_ref[g] = mm(jnp.concatenate([y, y], axis=1), sums_rhs(top, lag, lag, top), 1, 1)
    rate_two = by_lane(rate_ref[...])
    span = jnp.exp(-float(BLK) * rate_two)
    lane = lanes((1, BLK))
    low = lane < poles
    for g in range(groups):
        step = span[g : g + 1, :]
        couple = jnp.where(lane >= poles, float(BLK) * step, 0.0)
        state = jnp.zeros((width, BLK), F32)
        twin = jnp.zeros((width, BLK), F32)
        res_sum = jnp.zeros((width, BLK), F32)
        rate_sum = jnp.zeros((width, BLK), F32)
        for b in reversed(range(blocks)):
            at = slice(b * width, (b + 1) * width)
            rs_ref[g, at, :] = state
            first, second = sums_ref[g, at, :BLK], sums_ref[g, at, BLK:]
            before = states_ref[g, at, :]
            res_sum = res_sum + jnp.where(low, first * before, 0.0)
            rate_sum = rate_sum + (second + jnp.where(low, first, 0.0)) * before
            state, twin = (
                step * state + couple * twin + first,
                step * twin + jnp.where(low, 0.0, second),
            )
        fin_ref[g * width : (g + 1) * width, :] = state
        decay = jnp.exp(-rate_two[g : g + 1, :])
        cross_ref[0, g * width : (g + 1) * width, :] = decay * res_sum
        cross_ref[1, g * width : (g + 1) * width, :] = decay * rate_sum
    causal = rows((BLK, BLK)) >= lanes((BLK, BLK))
    for g in range(groups):
        own = slice(g * poles, (g + 1) * poles)
        y = stacked(gt_ref, g, width, blocks)
        taps = mm(
            jnp.concatenate([u_hi[own], u_hi[own], u_lo[own]], axis=0),
            jnp.concatenate([v_hi[own], v_lo[own], v_hi[own]], axis=0),
            0,
            0,
        )
        taps = jnp.where(causal, taps, 0.0).astype(BF16)
        out = with_states(y, taps, rs_ref[g], trail[0][own], trail[1][own])
        for b in range(blocks):
            bt_ref[g * width : (g + 1) * width, b * BLK : (b + 1) * BLK] = out[
                b * width : (b + 1) * width
            ]
        x = stacked(xt_ref, g, width, blocks)
        pairs = jnp.where(causal, mm(y, x, 0, 0), 0.0).astype(BF16)
        rhs = jnp.concatenate(
            [
                jnp.concatenate([v_hi[own], v_lo[own]], axis=1),
                jnp.concatenate([w_hi[own], w_lo[own]], axis=1),
                jnp.zeros((BLK - 2 * poles, 2 * BLK), BF16),
            ],
            axis=0,
        )
        held = mm(jnp.concatenate([pairs, pairs], axis=1), rhs, 1, 1)
        since = rows((BLK, BLK)) - 64.0
        held = held * jnp.exp(-rate_two[g : g + 1, :] * since)
        res_row = jnp.sum(jnp.where(low, held, 0.0), axis=0, keepdims=True)
        rate_row = jnp.sum(jnp.where(low, since * held, -held), axis=0, keepdims=True)
        one = slice(g * width, g * width + 1)
        cross_ref[0, one, :] = cross_ref[0, one, :] + res_row
        cross_ref[1, one, :] = cross_ref[1, one, :] + rate_row
    starts = fin_ref[...].T
    start, start_lag = starts[:poles], starts[poles : 2 * poles]
    state_in, slope_in = in_ref[:poles, :], in_ref[poles:, :]
    decay = jnp.exp(-by_channel(rate_ref[...], channels))
    res_cross = cross_ref[0].T[:poles]
    rate_cross = cross_ref[1].T
    pay_ref[:poles, :] = start
    pay_ref[poles : 2 * poles, :] = res_cross + decay * start * state_in
    pay_ref[2 * poles :, :] = (
        rate_cross[:poles]
        + rate_cross[poles : 2 * poles]
        + decay * ((start_lag + start) * state_in + start * slope_in)
    )
    for b in range(blocks):
        at = slice(b * BLK, (b + 1) * BLK)
        back_ref[at, :] = bt_ref[:, at].T


def leave_kernel(
    here_ref, all_ref, back_ref, key_ref, value_ref, rate_ref, res_ref, dk_ref, dv_ref, dres_ref, drate_ref
):
    tokens, channels = back_ref.shape
    groups, poles = rate_ref.shape
    mine = 2 * here_ref[0] + here_ref[1]
    count = all_ref.shape[0]
    rate_nc = by_channel(rate_ref[...], channels)
    rate_row, res_row = by_column(rate_ref[...]).T, by_column(res_ref[...]).T
    state = jnp.zeros((poles, channels), F32)
    total = jnp.zeros((2 * poles, channels), F32)
    for place in range(count):
        gap = (place - 1 - mine).astype(F32)
        lag = jnp.maximum(gap, 0.0) * float(tokens)
        weight = jnp.where(gap >= 0.0, jnp.exp(-rate_nc * lag), 0.0)
        state = state + weight * all_ref[place, :poles, :]
        total = total + all_ref[place, poles:, :]
    tall = spread(state, groups)
    scale = 1.0 / float(tokens * count)
    both = exact(indicator(groups, channels), total, 1, 1)
    dres_ref[...] = both[:, :poles] * scale
    drate_ref[...] = -res_ref[...] * both[:, poles:] * scale
    for b in range(tokens // BLK):
        at = slice(b * BLK, (b + 1) * BLK)
        time = float(tokens - b * BLK) - rows((BLK, groups * poles))
        trail = res_row * jnp.exp(-rate_row * time)
        back = back_ref[at, :] + modes(trail, tall)
        dk_ref[at, :] = (back * value_ref[at, :].astype(F32)).astype(BF16)
        dv_ref[at, :] = (back * key_ref[at, :].astype(F32)).astype(BF16)


def block_copies(z, refs, to_ref, sem):
    own, r1, l1, r2, l2, r3, l3, r4, l4 = refs
    half = r4.shape[0]
    whole = ((0, own), (-1, r1), (1, l1), (-2, r2), (2, l2), (-3, r3), (3, l3))
    nz = len(whole) + 1
    for far, ref in whole:
        at = lax.rem(z + far + nz, nz)
        yield at, ref, lambda slot: to_ref.at[slot], lambda slot: sem.at[slot, 0]
    at = lax.rem(z + nz // 2, nz)
    yield at, r4, lambda slot: to_ref.at[slot, pl.ds(0, half), :], lambda slot: sem.at[slot, 0]
    yield at, l4, lambda slot: to_ref.at[slot, pl.ds(half, half), :], lambda slot: sem.at[slot, 1]


def fetch_half(z, which, refs, half_ref, sem):
    count = half_ref.shape[0]
    far_slot = lax.rem(z + count, count)
    far_here = lax.div(lax.rem(z + count, 2 * count), count) == which
    for at, ref, place, signal in block_copies(z, refs, half_ref, sem):
        slot = lax.rem(at, count)

        @pl.when(lax.div(at, count) == which)
        def _():
            pltpu.make_async_copy(ref, place(slot), signal(slot)).start()

    def wait(j):
        split_here = jnp.logical_and(far_here, far_slot == j)
        tokens = half_ref.shape[1]

        @pl.when(split_here)
        def _():
            for part in range(2):
                piece = half_ref.at[j, pl.ds(part * (tokens // 2), tokens // 2), :]
                pltpu.make_async_copy(piece, piece, sem.at[j, part]).wait()

        @pl.when(jnp.logical_not(split_here))
        def _():
            pltpu.make_async_copy(half_ref.at[j], half_ref.at[j], sem.at[j, 0]).wait()

    return wait


def away_kernel(here_ref, *refs):
    blocks, gates, (away_ref, half_ref, sem) = refs[:9], refs[9:13], refs[13:]
    count, _, width = half_ref.shape
    wait = fetch_half(here_ref[2], 1 - here_ref[1], blocks, half_ref, sem)
    for j in range(count):
        wait(j)
        at = slice(j * width, (j + 1) * width)
        for i, gate in enumerate(gates):
            away_ref[i, :, at] = mm(gate[...], half_ref[j]).astype(BF16)


def project_kernel(here_ref, *refs):
    blocks, weights_ref, outs, (f_ref, w_ref, f_sem, w_sem) = refs[:9], refs[9], refs[10:14], refs[14:]
    z, x = here_ref[2], here_ref[3]
    nz, tokens, _ = f_ref.shape
    nx = weights_ref.shape[0]
    feat = [
        pltpu.make_async_copy(ref, place(at), signal(at))
        for at, ref, place, signal in block_copies(z, blocks, f_ref, f_sem)
    ]
    order = (2, 1, 3, 0)
    weight = {}
    for i in order:
        at = lax.rem(x - i + nx, nx)
        weight[i] = pltpu.make_async_copy(weights_ref.at[at], w_ref.at[i], w_sem.at[i])
    for copy in [weight[order[0]]] + feat + [weight[i] for i in order[1:]]:
        copy.start()
    for copy in feat:
        copy.wait()
    tile = TILE
    for i in order:
        weight[i].wait()
        for m in range(tokens // tile):
            at = slice(m * tile, (m + 1) * tile)
            lhs = jnp.concatenate([f_ref[j, at, :] for j in range(nz)], axis=1)
            outs[i][at, :] = mm(lhs, w_ref[i]).astype(BF16)


def chip_kernel(here_ref, *refs):
    blocks, came_ref, gates, outs, (gate_ref, half_ref, sem) = refs[:9], refs[9], refs[10:14], refs[14:18], refs[18:]
    y, core = here_ref[0], here_ref[1]
    count, _, width = half_ref.shape
    wait = fetch_half(here_ref[2], core, blocks, half_ref, sem)
    for i, gate in enumerate(gates):
        gate_ref[i] = gate[...]
    for j in range(count):
        wait(j)
        at = slice(j * width, (j + 1) * width)
        for r, out in enumerate(outs):
            i = lax.rem(8 - y - r, 4)
            part = mm(gate_ref[i], half_ref[j])
            out[:, at] = (part + came_ref[i, :, at].astype(F32)).astype(BF16)


def column_kernel(a_ref, b_ref, c_ref, d_ref, out_ref):
    total = (a_ref[...].astype(F32) + b_ref[...].astype(F32)) + (
        c_ref[...].astype(F32) + d_ref[...].astype(F32)
    )
    out_ref[...] = total.astype(BF16)


def total_kernel(scale, in_ref, out_ref):
    for b in range(in_ref.shape[1] // BLK):
        at = slice(b * BLK, (b + 1) * BLK)
        out_ref[at, :] = in_ref[:, at].astype(F32).T * scale


MIB = 2**20


def call(kernel, outs, scratch, ops, vmem, us, scalars=0, far=()):
    spec = pl.BlockSpec(memory_space=pltpu.VMEM)
    return pl.pallas_call(
        kernel,
        out_shape=outs,
        in_specs=[
            pl.BlockSpec(memory_space=pltpu.SMEM)
            if i < scalars
            else (pl.BlockSpec(memory_space=pltpu.HBM) if i in far else spec)
            for i in range(len(ops))
        ],
        out_specs=[spec] * len(outs),
        scratch_shapes=scratch,
        compiler_params=pltpu.CompilerParams(vmem_limit_bytes=vmem * MIB),
        cost_estimate=pl.CostEstimate(
            flops=1000, bytes_accessed=int(us * 3.69e6), transcendentals=0
        ),
    )(*ops)


def shift(n, by):
    return [(i, (i + by) % n) for i in range(n)]


def gather_ctx(item):
    n = lax.axis_size(CTX)
    return lax.all_to_all(
        jnp.broadcast_to(item[None], (n,) + item.shape), CTX, split_axis=0, concat_axis=0
    )


def after(value, *others):
    return lax.optimization_barrier((value, others))[0]


def local(query, key, value, out_grad, out_weight, rate, residue):
    tokens, channels = query.shape
    groups, poles = rate.shape
    feats = out_weight.shape[0]
    y, core = lax.axis_index("y"), lax.axis_index("core")
    x, z = lax.axis_index("x"), lax.axis_index("z")
    nx, ny, nz = lax.axis_size("x"), lax.axis_size("y"), lax.axis_size("z")
    here = jnp.stack([y, core, z, x]).astype(jnp.int32)
    swap = [(0, 1), (1, 0)]
    sds = jax.ShapeDtypeStruct
    half_scratch = [
        pltpu.VMEM((nz // 2, tokens, channels), BF16),
        pltpu.SemaphoreType.DMA((nz // 2, 2)),
    ]
    stack_shape = (groups, tokens // BLK * (channels // groups))

    def both_ways(axis, pair):
        n = lax.axis_size(axis)
        return (
            lax.ppermute(pair[0], axis, shift(n, 1)),
            lax.ppermute(pair[1], axis, shift(n, -1)),
        )

    rows_x = feats // nx
    half_rows = rows_x // 2
    weights = lax.all_to_all(
        out_weight.reshape(nx, rows_x, channels), "x", split_axis=0, concat_axis=0
    )

    hop1 = both_ways("z", (out_grad, out_grad))

    conv_own, ends, xt, states = call(
        forward_kernel,
        [
            sds((tokens, channels), F32),
            sds((2 * poles, channels), F32),
            sds((channels, tokens), BF16),
            sds(stack_shape + (BLK,), F32),
        ],
        [
            pltpu.VMEM((channels, tokens), F32),
            pltpu.VMEM(stack_shape + (2 * BLK,), F32),
            pltpu.VMEM((channels, BLK), F32),
        ],
        [key, value, rate, residue],
        12,
        10.0,
    )
    other_ends = lax.ppermute(ends, "core", swap)
    pair = jnp.stack([ends, other_ends])
    hop2 = both_ways("z", after(hop1, ends))
    all_ends = [ends, other_ends] + [
        lax.ppermute(pair, "y", shift(ny, i)) for i in range(1, ny)
    ]
    conv, gated, entering = call(
        enter_kernel,
        [
            sds((tokens, channels), F32),
            sds((channels, tokens), BF16),
            sds((2 * poles, channels), F32),
        ],
        [],
        [here] + all_ends + [after(conv_own, hop2), query, rate, residue],
        8,
        10.0,
        scalars=1,
    )
    hop3 = both_ways("z", after(hop2, all_ends))
    gates = [gated] + [lax.ppermute(gated, "x", shift(nx, i)) for i in range(1, nx)]
    right, left = after(hop3, gated)
    hop4 = both_ways("z", (right[: tokens // 2], left[tokens // 2 :]))
    blocks = [out_grad, *hop1, *hop2, *hop3, *hop4]

    own, one, two, three = call(
        project_kernel,
        [sds((tokens, channels), BF16)] * nx,
        [
            pltpu.VMEM((nz, tokens, channels), BF16),
            pltpu.VMEM((nx, rows_x, channels), BF16),
            pltpu.SemaphoreType.DMA((nz, 2)),
            pltpu.SemaphoreType.DMA((nx,)),
        ],
        [here] + blocks + [weights],
        16,
        6.0,
        scalars=1,
        far=tuple(range(1, 11)),
    )
    sums = [
        lax.ppermute(part, "x", shift(nx, -i)) for i, part in ((2, two), (1, one), (3, three))
    ]

    (away,) = call(
        away_kernel,
        [sds((nx, channels, half_rows), BF16)],
        half_scratch,
        [here] + after(blocks, own) + gates,
        12,
        0.5,
        scalars=1,
        far=tuple(range(1, 10)),
    )
    came = lax.ppermute(away, "core", swap)

    chip = call(
        chip_kernel,
        [sds((channels, half_rows), BF16)] * nx,
        [pltpu.VMEM((nx, channels, tokens), BF16)] + half_scratch,
        [here] + blocks + [came] + gates,
        16,
        0.5,
        scalars=1,
        far=tuple(range(1, 10)),
    )
    parts = [chip[0]] + [lax.ppermute(chip[r], "y", shift(ny, r)) for r in range(1, ny)]
    d_query, back_own, pay = call(
        backward_kernel,
        [
            sds((tokens, channels), BF16),
            sds((tokens, channels), F32),
            sds((3 * poles, channels), F32),
        ],
        [
            pltpu.VMEM((channels, tokens), BF16),
            pltpu.VMEM((channels, tokens), F32),
            pltpu.VMEM(stack_shape + (2 * BLK,), F32),
            pltpu.VMEM(stack_shape + (BLK,), F32),
            pltpu.VMEM((channels, BLK), F32),
            pltpu.VMEM((2, channels, BLK), F32),
        ],
        [after(own, chip)] + sums + [query, conv, xt, states, entering, rate, residue],
        16,
        20.0,
    )
    parts[0] = after(parts[0], pay)
    (column,) = call(column_kernel, [sds((channels, half_rows), BF16)], [], parts, 8, 1.0)
    all_pay = gather_ctx(after(pay, column))
    route = [(a * nx + b, b * nx + (a + b) % nx) for a in range(ny) for b in range(nx)]
    column = lax.ppermute(column, ("y", "x"), route)

    d_key, d_value, d_residue, d_rate = call(
        leave_kernel,
        [
            sds((tokens, channels), BF16),
            sds((tokens, channels), BF16),
            sds((groups, poles), F32),
            sds((groups, poles), F32),
        ],
        [],
        [here, all_pay, back_own, key, value, rate, residue],
        8,
        2.5,
        scalars=1,
    )
    (d_weight,) = call(
        functools.partial(total_kernel, 1.0 / float(tokens * 2 * nx)),
        [sds((half_rows, channels), F32)],
        [],
        [column],
        8,
        1.5,
    )
    return (d_query, d_key, d_value, d_weight, d_residue, d_rate)


def solution(mesh):
    fine = Mesh(mesh.devices.reshape(4, 2, 4, 8), ("y", "core", "x", "z"))
    both = P(CTX, CHAN)
    param = P(CHAN, None)
    return jax.shard_map(
        local,
        mesh=fine,
        in_specs=(both, both, both, both, P(None, CHAN), param, param),
        out_specs=(both, both, both, both, param, param),
        check_vma=False,
    )
```

```python
import functools

import jax
import jax.numpy as jnp
from jax import lax
from jax.experimental import pallas as pl
from jax.experimental.pallas import tpu as pltpu
from jax.sharding import Mesh
from jax.sharding import PartitionSpec as P

BLK = 128
TILE = 256
F32 = jnp.float32
BF16 = jnp.bfloat16
VMEM_LIMIT = 56 * 1024 * 1024
CTX = ("y", "core")
CHAN = ("x", "z")


def split(x):
    hi = x.astype(BF16)
    return hi, (x - hi.astype(F32)).astype(BF16)


def mm(a, b, ca=1, cb=0):
    return lax.dot_general(a, b, (((ca,), (cb,)), ((), ())), preferred_element_type=F32)


def lanes(shape):
    return lax.broadcasted_iota(jnp.int32, shape, 1).astype(F32)


def rows(shape):
    return lax.broadcasted_iota(jnp.int32, shape, 0).astype(F32)


def exact(a, b, ca, cb):
    return lax.dot_general(
        a, b, (((ca,), (cb,)), ((), ())), preferred_element_type=F32, precision=lax.Precision.HIGHEST
    )


def by_column(param):
    turned = param.T
    groups, poles = param.shape
    return jnp.concatenate(
        [jnp.broadcast_to(turned[:, g : g + 1], (poles, BLK)) for g in range(groups)], axis=0
    )


def by_lane(param):
    groups, poles = param.shape
    return jnp.concatenate([param, param, jnp.zeros((groups, BLK - 2 * poles), F32)], axis=1)


def indicator(groups, channels):
    shape = (groups, channels)
    return (
        lax.broadcasted_iota(jnp.int32, shape, 0)
        == lax.broadcasted_iota(jnp.int32, shape, 1) // (channels // groups)
    ).astype(F32)


def by_channel(param, channels):
    return exact(param, indicator(param.shape[0], channels), 0, 0)


def stacked(ref, g, width, blocks):
    return jnp.concatenate(
        [ref[g * width : (g + 1) * width, b * BLK : (b + 1) * BLK] for b in range(blocks)], axis=0
    )


def with_states(x, taps, state, lead_hi, lead_lo):
    poles = lead_hi.shape[0]
    none = jnp.zeros((BLK - poles, BLK), BF16)
    s_hi, s_lo = split(state)
    first = mm(
        jnp.concatenate([x, s_hi], axis=1), jnp.concatenate([taps, lead_hi, none], axis=0)
    )
    second = mm(
        jnp.concatenate([s_lo, s_hi], axis=1),
        jnp.concatenate([lead_hi, none, lead_lo, none], axis=0),
    )
    return first + second


def sums_rhs(top, second, third, fourth):
    poles = top[0].shape[0]
    none = jnp.zeros((poles, 2 * BLK), BF16)
    rest = jnp.zeros((BLK - 2 * poles, 2 * BLK), BF16)

    def part(pair):
        return none if pair is None else jnp.concatenate(pair, axis=1)

    return jnp.concatenate(
        [part(top), part(second), rest, part(third), part(fourth), rest], axis=0
    )


def forward_kernel(
    key_ref, value_ref, rate_ref, res_ref, conv_ref, ends_ref, xt_ref, states_ref, ct_ref, sums_ref, fin_ref
):
    tokens, channels = key_ref.shape
    groups, poles = rate_ref.shape
    width, blocks = channels // groups, tokens // BLK
    for b in range(blocks):
        at = slice(b * BLK, (b + 1) * BLK)
        inner = key_ref[at, :].astype(F32) * value_ref[at, :].astype(F32)
        xt_ref[:, at] = inner.T.astype(BF16)
    rate, res = by_column(rate_ref[...]), by_column(res_ref[...])
    time = lanes(rate.shape)
    u_hi, u_lo = split(res * jnp.exp(-rate * (time - 64.0)))
    v_hi, v_lo = split(jnp.exp(rate * (time - 64.0)))
    tail_all = jnp.exp(-rate * (BLK - 1.0 - time))
    tail = split(tail_all)
    tail_lag = split((BLK - 1.0 - time) * tail_all)
    lead = split(res * jnp.exp(-rate * (time + 1.0)))
    for g in range(groups):
        own = slice(g * poles, (g + 1) * poles)
        x = stacked(xt_ref, g, width, blocks)
        top = tuple(part[own] for part in tail)
        lag = tuple(part[own] for part in tail_lag)
        sums_ref[g] = mm(
            jnp.concatenate([x, x], axis=1), sums_rhs(top, lag, None, top), 1, 1
        )
    rate_two = by_lane(rate_ref[...])
    span = jnp.exp(-float(BLK) * rate_two)
    lane = lanes((1, BLK))
    for g in range(groups):
        step = span[g : g + 1, :]
        couple = jnp.where(lane >= poles, float(BLK) * step, 0.0)
        state = jnp.zeros((width, BLK), F32)
        twin = jnp.zeros((width, BLK), F32)
        for b in range(blocks):
            at = slice(b * width, (b + 1) * width)
            states_ref[g, at, :] = state
            state = step * state + couple * twin + sums_ref[g, at, :BLK]
            twin = step * twin + sums_ref[g, at, BLK:]
        fin_ref[g * width : (g + 1) * width, :] = state
    ends_ref[...] = fin_ref[...].T[: 2 * poles, :]
    causal = lanes((BLK, BLK)) >= rows((BLK, BLK))
    for g in range(groups):
        own = slice(g * poles, (g + 1) * poles)
        x = stacked(xt_ref, g, width, blocks)
        taps = mm(
            jnp.concatenate([v_hi[own], v_lo[own], v_hi[own]], axis=0),
            jnp.concatenate([u_hi[own], u_hi[own], u_lo[own]], axis=0),
            0,
            0,
        )
        taps = jnp.where(causal, taps, 0.0).astype(BF16)
        out = with_states(x, taps, states_ref[g], lead[0][own], lead[1][own])
        for b in range(blocks):
            ct_ref[g * width : (g + 1) * width, b * BLK : (b + 1) * BLK] = out[
                b * width : (b + 1) * width
            ]
    for b in range(blocks):
        at = slice(b * BLK, (b + 1) * BLK)
        conv_ref[at, :] = ct_ref[:, at].T


def spread(state, groups):
    poles, channels = state.shape
    width = channels // groups
    tall = jnp.concatenate([state] * groups, axis=0)
    row = lax.broadcasted_iota(jnp.int32, tall.shape, 0) // poles
    col = lax.broadcasted_iota(jnp.int32, tall.shape, 1) // width
    return jnp.where(row == col, tall, 0.0)


def modes(lead, state_tall):
    l_hi, l_lo = split(lead)
    s_hi, s_lo = split(state_tall)
    return mm(l_hi, s_hi) + mm(l_hi, s_lo) + mm(l_lo, s_hi)


def arrived(y, core, own_ref, other_ref, pair_refs):
    count = len(pair_refs) + 1
    yield 2 * y + core, lambda lo, hi: own_ref[lo:hi, :]
    yield 2 * y + 1 - core, lambda lo, hi: other_ref[lo:hi, :]
    for i, ref in enumerate(pair_refs, 1):
        far = lax.rem(y - i + count, count)
        yield 2 * far + core, lambda lo, hi, ref=ref: ref[0, lo:hi, :]
        yield 2 * far + 1 - core, lambda lo, hi, ref=ref: ref[1, lo:hi, :]


def enter_kernel(
    here_ref, own_ref, other_ref, p1_ref, p2_ref, p3_ref, conv_ref, query_ref, rate_ref, res_ref, conv_out_ref, gated_ref, in_ref
):
    tokens, channels = conv_ref.shape
    groups, poles = rate_ref.shape
    y, core = here_ref[0], here_ref[1]
    mine = 2 * y + core
    rate_nc = by_channel(rate_ref[...], channels)
    rate_row, res_row = by_column(rate_ref[...]).T, by_column(res_ref[...]).T
    state = jnp.zeros((poles, channels), F32)
    slope = jnp.zeros((poles, channels), F32)
    for place, read in arrived(y, core, own_ref, other_ref, (p1_ref, p2_ref, p3_ref)):
        gap = (mine - 1 - place).astype(F32)
        lag = jnp.maximum(gap, 0.0) * float(tokens)
        weight = jnp.where(gap >= 0.0, jnp.exp(-rate_nc * lag), 0.0)
        end = read(0, poles)
        state = state + weight * end
        slope = slope + weight * (read(poles, 2 * poles) + lag * end)
    in_ref[:poles, :] = state
    in_ref[poles:, :] = slope
    tall = spread(state, groups)
    for b in range(tokens // BLK):
        at = slice(b * BLK, (b + 1) * BLK)
        time = rows((BLK, groups * poles)) + float(b * BLK + 1)
        lead = res_row * jnp.exp(-rate_row * time)
        conv = conv_ref[at, :] + modes(lead, tall)
        conv_out_ref[at, :] = conv
        gated_ref[:, at] = (query_ref[at, :].astype(F32) * conv).T.astype(BF16)


def backward_kernel(
    own_ref, p1_ref, p2_ref, p3_ref, query_ref, conv_ref, xt_ref, states_ref, in_ref, rate_ref, res_ref,
    dq_ref, back_ref, pay_ref, gt_ref, bt_ref, sums_ref, rs_ref, fin_ref, cross_ref
):
    tokens, channels = query_ref.shape
    groups, poles = rate_ref.shape
    width, blocks = channels // groups, tokens // BLK
    for b in range(blocks):
        at = slice(b * BLK, (b + 1) * BLK)
        total = (own_ref[at, :].astype(F32) + p1_ref[at, :].astype(F32)) + (
            p2_ref[at, :].astype(F32) + p3_ref[at, :].astype(F32)
        )
        grad = total.astype(BF16).astype(F32)
        dq_ref[at, :] = (grad * conv_ref[at, :]).astype(BF16)
        gt_ref[:, at] = (grad * query_ref[at, :].astype(F32)).T.astype(BF16)
    rate, res = by_column(rate_ref[...]), by_column(res_ref[...])
    time = lanes(rate.shape)
    u_hi, u_lo = split(res * jnp.exp(-rate * (time - 64.0)))
    v_all = jnp.exp(rate * (time - 64.0))
    v_hi, v_lo = split(v_all)
    w_hi, w_lo = split((time - 64.0) * v_all)
    head_all = jnp.exp(-rate * time)
    head = split(head_all)
    head_lag = split(time * head_all)
    trail = split(res * jnp.exp(-rate * (BLK - time)))
    for g in range(groups):
        own = slice(g * poles, (g + 1) * poles)
        y = stacked(gt_ref, g, width, blocks)
        top = tuple(part[own] for part in head)
        lag = tuple(part[own] for part in head_lag)
        sums_ref[g] = mm(jnp.concatenate([y, y], axis=1), sums_rhs(top, lag, lag, top), 1, 1)
    rate_two = by_lane(rate_ref[...])
    span = jnp.exp(-float(BLK) * rate_two)
    lane = lanes((1, BLK))
    low = lane < poles
    for g in range(groups):
        step = span[g : g + 1, :]
        couple = jnp.where(lane >= poles, float(BLK) * step, 0.0)
        state = jnp.zeros((width, BLK), F32)
        twin = jnp.zeros((width, BLK), F32)
        res_sum = jnp.zeros((width, BLK), F32)
        rate_sum = jnp.zeros((width, BLK), F32)
        for b in reversed(range(blocks)):
            at = slice(b * width, (b + 1) * width)
            rs_ref[g, at, :] = state
            first, second = sums_ref[g, at, :BLK], sums_ref[g, at, BLK:]
            before = states_ref[g, at, :]
            res_sum = res_sum + jnp.where(low, first * before, 0.0)
            rate_sum = rate_sum + (second + jnp.where(low, first, 0.0)) * before
            state, twin = (
                step * state + couple * twin + first,
                step * twin + jnp.where(low, 0.0, second),
            )
        fin_ref[g * width : (g + 1) * width, :] = state
        decay = jnp.exp(-rate_two[g : g + 1, :])
        cross_ref[0, g * width : (g + 1) * width, :] = decay * res_sum
        cross_ref[1, g * width : (g + 1) * width, :] = decay * rate_sum
    causal = rows((BLK, BLK)) >= lanes((BLK, BLK))
    for g in range(groups):
        own = slice(g * poles, (g + 1) * poles)
        y = stacked(gt_ref, g, width, blocks)
        taps = mm(
            jnp.concatenate([u_hi[own], u_hi[own], u_lo[own]], axis=0),
            jnp.concatenate([v_hi[own], v_lo[own], v_hi[own]], axis=0),
            0,
            0,
        )
        taps = jnp.where(causal, taps, 0.0).astype(BF16)
        out = with_states(y, taps, rs_ref[g], trail[0][own], trail[1][own])
        for b in range(blocks):
            bt_ref[g * width : (g + 1) * width, b * BLK : (b + 1) * BLK] = out[
                b * width : (b + 1) * width
            ]
        x = stacked(xt_ref, g, width, blocks)
        pairs = jnp.where(causal, mm(y, x, 0, 0), 0.0).astype(BF16)
        rhs = jnp.concatenate(
            [
                jnp.concatenate([v_hi[own], v_lo[own]], axis=1),
                jnp.concatenate([w_hi[own], w_lo[own]], axis=1),
                jnp.zeros((BLK - 2 * poles, 2 * BLK), BF16),
            ],
            axis=0,
        )
        held = mm(jnp.concatenate([pairs, pairs], axis=1), rhs, 1, 1)
        since = rows((BLK, BLK)) - 64.0
        held = held * jnp.exp(-rate_two[g : g + 1, :] * since)
        res_row = jnp.sum(jnp.where(low, held, 0.0), axis=0, keepdims=True)
        rate_row = jnp.sum(jnp.where(low, since * held, -held), axis=0, keepdims=True)
        one = slice(g * width, g * width + 1)
        cross_ref[0, one, :] = cross_ref[0, one, :] + res_row
        cross_ref[1, one, :] = cross_ref[1, one, :] + rate_row
    starts = fin_ref[...].T
    start, start_lag = starts[:poles], starts[poles : 2 * poles]
    state_in, slope_in = in_ref[:poles, :], in_ref[poles:, :]
    decay = jnp.exp(-by_channel(rate_ref[...], channels))
    res_cross = cross_ref[0].T[:poles]
    rate_cross = cross_ref[1].T
    res_sum = res_cross + decay * start * state_in
    rate_sum = (
        rate_cross[:poles]
        + rate_cross[poles : 2 * poles]
        + decay * ((start_lag + start) * state_in + start * slope_in)
    )
    both = exact(indicator(groups, channels), jnp.concatenate([res_sum, rate_sum], axis=0), 1, 1)
    both = jnp.concatenate([both, jnp.zeros((groups, BLK - 2 * poles), F32)], axis=1)
    pay_ref[:poles, :] = start
    pay_ref[poles:, :] = jnp.concatenate([both[: groups // 2], both[groups // 2 :]], axis=1)
    for b in range(blocks):
        at = slice(b * BLK, (b + 1) * BLK)
        back_ref[at, :] = bt_ref[:, at].T


def leave_kernel(
    here_ref, all_ref, back_ref, key_ref, value_ref, rate_ref, res_ref, dk_ref, dv_ref, dres_ref, drate_ref
):
    tokens, channels = back_ref.shape
    groups, poles = rate_ref.shape
    mine = 2 * here_ref[0] + here_ref[1]
    count = all_ref.shape[0]
    rate_nc = by_channel(rate_ref[...], channels)
    rate_row, res_row = by_column(rate_ref[...]).T, by_column(res_ref[...]).T
    state = jnp.zeros((poles, channels), F32)
    total = jnp.zeros((groups // 2, channels), F32)
    for place in range(count):
        gap = (place - 1 - mine).astype(F32)
        lag = jnp.maximum(gap, 0.0) * float(tokens)
        weight = jnp.where(gap >= 0.0, jnp.exp(-rate_nc * lag), 0.0)
        state = state + weight * all_ref[place, :poles, :]
        total = total + all_ref[place, poles:, :]
    tall = spread(state, groups)
    scale = 1.0 / float(tokens * count)
    both = jnp.concatenate([total[:, : 2 * poles], total[:, BLK : BLK + 2 * poles]], axis=0)
    dres_ref[...] = both[:, :poles] * scale
    drate_ref[...] = -res_ref[...] * both[:, poles:] * scale
    for b in range(tokens // BLK):
        at = slice(b * BLK, (b + 1) * BLK)
        time = float(tokens - b * BLK) - rows((BLK, groups * poles))
        trail = res_row * jnp.exp(-rate_row * time)
        back = back_ref[at, :] + modes(trail, tall)
        dk_ref[at, :] = (back * value_ref[at, :].astype(F32)).astype(BF16)
        dv_ref[at, :] = (back * key_ref[at, :].astype(F32)).astype(BF16)


def block_copies(z, refs, to_ref, sem):
    own, r1, l1, r2, l2, r3, l3, r4, l4 = refs
    half = r4.shape[0]
    whole = ((0, own), (-1, r1), (1, l1), (-2, r2), (2, l2), (-3, r3), (3, l3))
    nz = len(whole) + 1
    for far, ref in whole:
        at = lax.rem(z + far + nz, nz)
        yield at, ref, lambda slot: to_ref.at[slot], lambda slot: sem.at[slot, 0]
    at = lax.rem(z + nz // 2, nz)
    yield at, r4, lambda slot: to_ref.at[slot, pl.ds(0, half), :], lambda slot: sem.at[slot, 0]
    yield at, l4, lambda slot: to_ref.at[slot, pl.ds(half, half), :], lambda slot: sem.at[slot, 1]


def fetch_half(z, which, refs, half_ref, sem):
    count = half_ref.shape[0]
    far_slot = lax.rem(z + count, count)
    far_here = lax.div(lax.rem(z + count, 2 * count), count) == which
    for at, ref, place, signal in block_copies(z, refs, half_ref, sem):
        slot = lax.rem(at, count)

        @pl.when(lax.div(at, count) == which)
        def _():
            pltpu.make_async_copy(ref, place(slot), signal(slot)).start()

    def wait(j):
        split_here = jnp.logical_and(far_here, far_slot == j)
        tokens = half_ref.shape[1]

        @pl.when(split_here)
        def _():
            for part in range(2):
                piece = half_ref.at[j, pl.ds(part * (tokens // 2), tokens // 2), :]
                pltpu.make_async_copy(piece, piece, sem.at[j, part]).wait()

        @pl.when(jnp.logical_not(split_here))
        def _():
            pltpu.make_async_copy(half_ref.at[j], half_ref.at[j], sem.at[j, 0]).wait()

    return wait


def away_kernel(here_ref, *refs):
    blocks, gates, (away_ref, half_ref, sem) = refs[:9], refs[9:13], refs[13:]
    count, _, width = half_ref.shape
    wait = fetch_half(here_ref[2], 1 - here_ref[1], blocks, half_ref, sem)
    for j in range(count):
        wait(j)
        at = slice(j * width, (j + 1) * width)
        for i, gate in enumerate(gates):
            away_ref[i, :, at] = mm(gate[...], half_ref[j]).astype(BF16)


def project_kernel(here_ref, *refs):
    blocks, (mine_ref, other_ref), outs, (f_ref, w_ref, f_sem, w_sem) = refs[:9], refs[9:11], refs[11:15], refs[15:]
    core, z, x = here_ref[1], here_ref[2], here_ref[3]
    nz, tokens, _ = f_ref.shape
    nx, half, _ = mine_ref.shape
    feat = [
        pltpu.make_async_copy(ref, place(at), signal(at))
        for at, ref, place, signal in block_copies(z, blocks, f_ref, f_sem)
    ]
    order = (2, 1, 3, 0)
    weight = {}
    for i in order:
        at = lax.rem(x - i + nx, nx)
        weight[i] = [
            pltpu.make_async_copy(
                ref.at[at], w_ref.at[i, pl.ds(pl.multiple_of(first, half), half), :], w_sem.at[i, j]
            )
            for j, (ref, first) in enumerate(((mine_ref, core * half), (other_ref, (1 - core) * half)))
        ]
    for copy in weight[order[0]] + feat:
        copy.start()
    for i in order[1:]:
        for copy in weight[i]:
            copy.start()
    for copy in feat:
        copy.wait()
    tile = TILE
    for i in order:
        for copy in weight[i]:
            copy.wait()
        for m in range(tokens // tile):
            at = slice(m * tile, (m + 1) * tile)
            lhs = jnp.concatenate([f_ref[j, at, :] for j in range(nz)], axis=1)
            outs[i][at, :] = mm(lhs, w_ref[i]).astype(BF16)


def chip_kernel(here_ref, *refs):
    blocks, came_ref, gates, outs, (gate_ref, half_ref, sem) = refs[:9], refs[9], refs[10:14], refs[14:18], refs[18:]
    y, core = here_ref[0], here_ref[1]
    count, _, width = half_ref.shape
    wait = fetch_half(here_ref[2], core, blocks, half_ref, sem)
    for i, gate in enumerate(gates):
        gate_ref[i] = gate[...]
    for j in range(count):
        wait(j)
        at = slice(j * width, (j + 1) * width)
        for r, out in enumerate(outs):
            i = lax.rem(8 - y - r, 4)
            part = mm(gate_ref[i], half_ref[j])
            out[:, at] = (part + came_ref[i, :, at].astype(F32)).astype(BF16)


def column_kernel(a_ref, b_ref, c_ref, d_ref, out_ref):
    total = (a_ref[...].astype(F32) + b_ref[...].astype(F32)) + (
        c_ref[...].astype(F32) + d_ref[...].astype(F32)
    )
    out_ref[...] = total.astype(BF16)


def total_kernel(scale, in_ref, out_ref):
    for b in range(in_ref.shape[1] // BLK):
        at = slice(b * BLK, (b + 1) * BLK)
        out_ref[at, :] = in_ref[:, at].astype(F32).T * scale


MIB = 2**20


def call(kernel, outs, scratch, ops, vmem, us, scalars=0, far=()):
    spec = pl.BlockSpec(memory_space=pltpu.VMEM)
    return pl.pallas_call(
        kernel,
        out_shape=outs,
        in_specs=[
            pl.BlockSpec(memory_space=pltpu.SMEM)
            if i < scalars
            else (pl.BlockSpec(memory_space=pltpu.HBM) if i in far else spec)
            for i in range(len(ops))
        ],
        out_specs=[spec] * len(outs),
        scratch_shapes=scratch,
        compiler_params=pltpu.CompilerParams(vmem_limit_bytes=vmem * MIB),
        cost_estimate=pl.CostEstimate(
            flops=1000, bytes_accessed=int(us * 3.69e6), transcendentals=0
        ),
    )(*ops)


def shift(n, by):
    return [(i, (i + by) % n) for i in range(n)]


def gather_ctx(item):
    n = lax.axis_size(CTX)
    return lax.all_to_all(
        jnp.broadcast_to(item[None], (n,) + item.shape), CTX, split_axis=0, concat_axis=0
    )


def after(value, *others):
    return lax.optimization_barrier((value, others))[0]


def local(query, key, value, out_grad, out_weight, rate, residue):
    tokens, channels = query.shape
    groups, poles = rate.shape
    feats = out_weight.shape[0]
    y, core = lax.axis_index("y"), lax.axis_index("core")
    x, z = lax.axis_index("x"), lax.axis_index("z")
    nx, ny, nz = lax.axis_size("x"), lax.axis_size("y"), lax.axis_size("z")
    here = jnp.stack([y, core, z, x]).astype(jnp.int32)
    swap = [(0, 1), (1, 0)]
    sds = jax.ShapeDtypeStruct
    half_scratch = [
        pltpu.VMEM((nz // 2, tokens, channels), BF16),
        pltpu.SemaphoreType.DMA((nz // 2, 2)),
    ]
    stack_shape = (groups, tokens // BLK * (channels // groups))

    def both_ways(axis, pair):
        n = lax.axis_size(axis)
        return (
            lax.ppermute(pair[0], axis, shift(n, 1)),
            lax.ppermute(pair[1], axis, shift(n, -1)),
        )

    rows_x = feats // nx
    half_rows = rows_x // 2
    w_mine = lax.dynamic_index_in_dim(
        out_weight.reshape(nx, 2, half_rows, channels), core, 1, keepdims=False
    )
    w_mine = lax.all_to_all(w_mine, "x", split_axis=0, concat_axis=0)

    hop1 = both_ways("z", (out_grad, out_grad))

    conv_own, ends, xt, states = call(
        forward_kernel,
        [
            sds((tokens, channels), F32),
            sds((2 * poles, channels), F32),
            sds((channels, tokens), BF16),
            sds(stack_shape + (BLK,), F32),
        ],
        [
            pltpu.VMEM((channels, tokens), F32),
            pltpu.VMEM(stack_shape + (2 * BLK,), F32),
            pltpu.VMEM((channels, BLK), F32),
        ],
        [key, value, rate, residue],
        12,
        10.0,
    )
    other_ends = lax.ppermute(ends, "core", swap)
    pair = jnp.stack([ends, other_ends])
    hop2 = both_ways("z", after(hop1, ends))
    all_ends = [ends, other_ends] + [
        lax.ppermute(pair, "y", shift(ny, i)) for i in range(1, ny)
    ]
    conv, gated, entering = call(
        enter_kernel,
        [
            sds((tokens, channels), F32),
            sds((channels, tokens), BF16),
            sds((2 * poles, channels), F32),
        ],
        [],
        [here] + all_ends + [after(conv_own, hop2), query, rate, residue],
        8,
        10.0,
        scalars=1,
    )
    hop3 = both_ways("z", after(hop2, all_ends))
    w_other = lax.ppermute(after(w_mine, hop2, all_ends), "core", swap)
    sent = after(gated, w_other)
    gates = [gated] + [lax.ppermute(sent, "x", shift(nx, i)) for i in range(1, nx)]
    right, left = after(hop3, gated)
    hop4 = both_ways("z", (right[: tokens // 2], left[tokens // 2 :]))
    blocks = [out_grad, *hop1, *hop2, *hop3, *hop4]

    own, one, two, three = call(
        project_kernel,
        [sds((tokens, channels), BF16)] * nx,
        [
            pltpu.VMEM((nz, tokens, channels), BF16),
            pltpu.VMEM((nx, rows_x, channels), BF16),
            pltpu.SemaphoreType.DMA((nz, 2)),
            pltpu.SemaphoreType.DMA((nx, 2)),
        ],
        [here] + blocks + [w_mine, w_other],
        16,
        6.0,
        scalars=1,
        far=tuple(range(1, 12)),
    )
    sums = [
        lax.ppermute(part, "x", shift(nx, -i)) for i, part in ((2, two), (1, one), (3, three))
    ]

    (away,) = call(
        away_kernel,
        [sds((nx, channels, half_rows), BF16)],
        half_scratch,
        [here] + after(blocks, own) + gates,
        12,
        0.5,
        scalars=1,
        far=tuple(range(1, 10)),
    )
    came = lax.ppermute(away, "core", swap)

    chip = call(
        chip_kernel,
        [sds((channels, half_rows), BF16)] * nx,
        [pltpu.VMEM((nx, channels, tokens), BF16)] + half_scratch,
        [here] + blocks + [came] + gates,
        16,
        0.5,
        scalars=1,
        far=tuple(range(1, 10)),
    )
    parts = [chip[0]] + [lax.ppermute(chip[r], "y", shift(ny, r)) for r in range(1, ny)]
    d_query, back_own, pay = call(
        backward_kernel,
        [
            sds((tokens, channels), BF16),
            sds((tokens, channels), F32),
            sds((poles + groups // 2, channels), F32),
        ],
        [
            pltpu.VMEM((channels, tokens), BF16),
            pltpu.VMEM((channels, tokens), F32),
            pltpu.VMEM(stack_shape + (2 * BLK,), F32),
            pltpu.VMEM(stack_shape + (BLK,), F32),
            pltpu.VMEM((channels, BLK), F32),
            pltpu.VMEM((2, channels, BLK), F32),
        ],
        [after(own, chip)] + sums + [query, conv, xt, states, entering, rate, residue],
        16,
        20.0,
    )
    parts[0] = after(parts[0], pay)
    (column,) = call(column_kernel, [sds((channels, half_rows), BF16)], [], parts, 8, 1.0)
    all_pay = gather_ctx(pay)
    route = [(a * nx + b, b * nx + (a + b) % nx) for a in range(ny) for b in range(nx)]
    column = lax.ppermute(column, ("y", "x"), route)

    d_key, d_value, d_residue, d_rate = call(
        leave_kernel,
        [
            sds((tokens, channels), BF16),
            sds((tokens, channels), BF16),
            sds((groups, poles), F32),
            sds((groups, poles), F32),
        ],
        [],
        [here, all_pay, back_own, key, value, rate, residue],
        8,
        2.5,
        scalars=1,
    )
    (d_weight,) = call(
        functools.partial(total_kernel, 1.0 / float(tokens * 2 * nx)),
        [sds((half_rows, channels), F32)],
        [],
        [column],
        8,
        1.5,
    )
    return (d_query, d_key, d_value, d_weight, d_residue, d_rate)


def solution(mesh):
    fine = Mesh(mesh.devices.reshape(4, 2, 4, 8), ("y", "core", "x", "z"))
    both = P(CTX, CHAN)
    param = P(CHAN, None)
    return jax.shard_map(
        local,
        mesh=fine,
        in_specs=(both, both, both, both, P(None, CHAN), param, param),
        out_specs=(both, both, both, both, param, param),
        check_vma=False,
    )
```

```python
import functools

import jax
import jax.numpy as jnp
from jax import lax
from jax.experimental import pallas as pl
from jax.experimental.pallas import tpu as pltpu
from jax.sharding import Mesh
from jax.sharding import PartitionSpec as P

BLK = 128
TILE = 256
F32 = jnp.float32
BF16 = jnp.bfloat16
VMEM_LIMIT = 56 * 1024 * 1024
CTX = ("y", "core")
CHAN = ("x", "z")


def split(x):
    hi = x.astype(BF16)
    return hi, (x - hi.astype(F32)).astype(BF16)


def mm(a, b, ca=1, cb=0):
    return lax.dot_general(a, b, (((ca,), (cb,)), ((), ())), preferred_element_type=F32)


def lanes(shape):
    return lax.broadcasted_iota(jnp.int32, shape, 1).astype(F32)


def rows(shape):
    return lax.broadcasted_iota(jnp.int32, shape, 0).astype(F32)


def exact(a, b, ca, cb):
    return lax.dot_general(
        a, b, (((ca,), (cb,)), ((), ())), preferred_element_type=F32, precision=lax.Precision.HIGHEST
    )


def by_column(param):
    turned = param.T
    groups, poles = param.shape
    return jnp.concatenate(
        [jnp.broadcast_to(turned[:, g : g + 1], (poles, BLK)) for g in range(groups)], axis=0
    )


def by_lane(param):
    groups, poles = param.shape
    return jnp.concatenate([param, param, jnp.zeros((groups, BLK - 2 * poles), F32)], axis=1)


def indicator(groups, channels):
    shape = (groups, channels)
    return (
        lax.broadcasted_iota(jnp.int32, shape, 0)
        == lax.broadcasted_iota(jnp.int32, shape, 1) // (channels // groups)
    ).astype(F32)


def by_channel(param, channels):
    return exact(param, indicator(param.shape[0], channels), 0, 0)


def stacked(ref, g, width, blocks):
    return jnp.concatenate(
        [ref[g * width : (g + 1) * width, b * BLK : (b + 1) * BLK] for b in range(blocks)], axis=0
    )


def with_states(x, taps, state, lead_hi, lead_lo):
    poles = lead_hi.shape[0]
    none = jnp.zeros((BLK - poles, BLK), BF16)
    s_hi, s_lo = split(state)
    first = mm(
        jnp.concatenate([x, s_hi], axis=1), jnp.concatenate([taps, lead_hi, none], axis=0)
    )
    second = mm(
        jnp.concatenate([s_lo, s_hi], axis=1),
        jnp.concatenate([lead_hi, none, lead_lo, none], axis=0),
    )
    return first + second


def sums_rhs(top, second, third, fourth):
    poles = top[0].shape[0]
    none = jnp.zeros((poles, 2 * BLK), BF16)
    rest = jnp.zeros((BLK - 2 * poles, 2 * BLK), BF16)

    def part(pair):
        return none if pair is None else jnp.concatenate(pair, axis=1)

    return jnp.concatenate(
        [part(top), part(second), rest, part(third), part(fourth), rest], axis=0
    )


def forward_kernel(
    key_ref, value_ref, rate_ref, res_ref, conv_ref, ends_ref, xt_ref, states_ref, ct_ref, sums_ref, fin_ref
):
    tokens, channels = key_ref.shape
    groups, poles = rate_ref.shape
    width, blocks = channels // groups, tokens // BLK
    for b in range(blocks):
        at = slice(b * BLK, (b + 1) * BLK)
        inner = key_ref[at, :].astype(F32) * value_ref[at, :].astype(F32)
        xt_ref[:, at] = inner.T.astype(BF16)
    rate, res = by_column(rate_ref[...]), by_column(res_ref[...])
    time = lanes(rate.shape)
    u_hi, u_lo = split(res * jnp.exp(-rate * (time - 64.0)))
    v_hi, v_lo = split(jnp.exp(rate * (time - 64.0)))
    tail_all = jnp.exp(-rate * (BLK - 1.0 - time))
    tail = split(tail_all)
    tail_lag = split((BLK - 1.0 - time) * tail_all)
    lead = split(res * jnp.exp(-rate * (time + 1.0)))
    for g in range(groups):
        own = slice(g * poles, (g + 1) * poles)
        x = stacked(xt_ref, g, width, blocks)
        top = tuple(part[own] for part in tail)
        lag = tuple(part[own] for part in tail_lag)
        sums_ref[g] = mm(
            jnp.concatenate([x, x], axis=1), sums_rhs(top, lag, None, top), 1, 1
        )
    rate_two = by_lane(rate_ref[...])
    span = jnp.exp(-float(BLK) * rate_two)
    lane = lanes((1, BLK))
    for g in range(groups):
        step = span[g : g + 1, :]
        couple = jnp.where(lane >= poles, float(BLK) * step, 0.0)
        state = jnp.zeros((width, BLK), F32)
        twin = jnp.zeros((width, BLK), F32)
        for b in range(blocks):
            at = slice(b * width, (b + 1) * width)
            states_ref[g, at, :] = state
            state = step * state + couple * twin + sums_ref[g, at, :BLK]
            twin = step * twin + sums_ref[g, at, BLK:]
        fin_ref[g * width : (g + 1) * width, :] = state
    ends_ref[...] = fin_ref[...].T[: 2 * poles, :]
    causal = lanes((BLK, BLK)) >= rows((BLK, BLK))
    for g in range(groups):
        own = slice(g * poles, (g + 1) * poles)
        x = stacked(xt_ref, g, width, blocks)
        taps = mm(
            jnp.concatenate([v_hi[own], v_lo[own], v_hi[own]], axis=0),
            jnp.concatenate([u_hi[own], u_hi[own], u_lo[own]], axis=0),
            0,
            0,
        )
        taps = jnp.where(causal, taps, 0.0).astype(BF16)
        out = with_states(x, taps, states_ref[g], lead[0][own], lead[1][own])
        for b in range(blocks):
            ct_ref[g * width : (g + 1) * width, b * BLK : (b + 1) * BLK] = out[
                b * width : (b + 1) * width
            ]
    for b in range(blocks):
        at = slice(b * BLK, (b + 1) * BLK)
        conv_ref[at, :] = ct_ref[:, at].T


def spread(state, groups):
    poles, channels = state.shape
    width = channels // groups
    tall = jnp.concatenate([state] * groups, axis=0)
    row = lax.broadcasted_iota(jnp.int32, tall.shape, 0) // poles
    col = lax.broadcasted_iota(jnp.int32, tall.shape, 1) // width
    return jnp.where(row == col, tall, 0.0)


def modes(lead, state_tall):
    l_hi, l_lo = split(lead)
    s_hi, s_lo = split(state_tall)
    return mm(l_hi, s_hi) + mm(l_hi, s_lo) + mm(l_lo, s_hi)


def arrived(y, core, own_ref, other_ref, pair_refs):
    count = len(pair_refs) + 1
    yield 2 * y + core, lambda lo, hi: own_ref[lo:hi, :]
    yield 2 * y + 1 - core, lambda lo, hi: other_ref[lo:hi, :]
    for i, ref in enumerate(pair_refs, 1):
        far = lax.rem(y - i + count, count)
        yield 2 * far + core, lambda lo, hi, ref=ref: ref[0, lo:hi, :]
        yield 2 * far + 1 - core, lambda lo, hi, ref=ref: ref[1, lo:hi, :]


def enter_kernel(
    here_ref, own_ref, other_ref, p1_ref, p2_ref, p3_ref, conv_ref, query_ref, rate_ref, res_ref, conv_out_ref, gated_ref, in_ref
):
    tokens, channels = conv_ref.shape
    groups, poles = rate_ref.shape
    y, core = here_ref[0], here_ref[1]
    mine = 2 * y + core
    rate_nc = by_channel(rate_ref[...], channels)
    rate_row, res_row = by_column(rate_ref[...]).T, by_column(res_ref[...]).T
    state = jnp.zeros((poles, channels), F32)
    slope = jnp.zeros((poles, channels), F32)
    for place, read in arrived(y, core, own_ref, other_ref, (p1_ref, p2_ref, p3_ref)):
        gap = (mine - 1 - place).astype(F32)
        lag = jnp.maximum(gap, 0.0) * float(tokens)
        weight = jnp.where(gap >= 0.0, jnp.exp(-rate_nc * lag), 0.0)
        end = read(0, poles)
        state = state + weight * end
        slope = slope + weight * (read(poles, 2 * poles) + lag * end)
    in_ref[:poles, :] = state
    in_ref[poles:, :] = slope
    tall = spread(state, groups)
    for b in range(tokens // BLK):
        at = slice(b * BLK, (b + 1) * BLK)
        time = rows((BLK, groups * poles)) + float(b * BLK + 1)
        lead = res_row * jnp.exp(-rate_row * time)
        conv = conv_ref[at, :] + modes(lead, tall)
        conv_out_ref[at, :] = conv
        gated_ref[:, at] = (query_ref[at, :].astype(F32) * conv).T.astype(BF16)


def backward_kernel(
    own_ref, p1_ref, p2_ref, p3_ref, query_ref, conv_ref, xt_ref, states_ref, in_ref, rate_ref, res_ref,
    dq_ref, back_ref, pay_ref, gt_ref, bt_ref, sums_ref, rs_ref, fin_ref, cross_ref
):
    tokens, channels = query_ref.shape
    groups, poles = rate_ref.shape
    width, blocks = channels // groups, tokens // BLK
    for b in range(blocks):
        at = slice(b * BLK, (b + 1) * BLK)
        total = (own_ref[at, :].astype(F32) + p1_ref[at, :].astype(F32)) + (
            p2_ref[at, :].astype(F32) + p3_ref[at, :].astype(F32)
        )
        grad = total.astype(BF16).astype(F32)
        dq_ref[at, :] = (grad * conv_ref[at, :]).astype(BF16)
        gt_ref[:, at] = (grad * query_ref[at, :].astype(F32)).T.astype(BF16)
    rate, res = by_column(rate_ref[...]), by_column(res_ref[...])
    time = lanes(rate.shape)
    u_hi, u_lo = split(res * jnp.exp(-rate * (time - 64.0)))
    v_all = jnp.exp(rate * (time - 64.0))
    v_hi, v_lo = split(v_all)
    w_hi, w_lo = split((time - 64.0) * v_all)
    head_all = jnp.exp(-rate * time)
    head = split(head_all)
    head_lag = split(time * head_all)
    trail = split(res * jnp.exp(-rate * (BLK - time)))
    for g in range(groups):
        own = slice(g * poles, (g + 1) * poles)
        y = stacked(gt_ref, g, width, blocks)
        top = tuple(part[own] for part in head)
        lag = tuple(part[own] for part in head_lag)
        sums_ref[g] = mm(jnp.concatenate([y, y], axis=1), sums_rhs(top, lag, lag, top), 1, 1)
    rate_two = by_lane(rate_ref[...])
    span = jnp.exp(-float(BLK) * rate_two)
    lane = lanes((1, BLK))
    low = lane < poles
    for g in range(groups):
        step = span[g : g + 1, :]
        couple = jnp.where(lane >= poles, float(BLK) * step, 0.0)
        state = jnp.zeros((width, BLK), F32)
        twin = jnp.zeros((width, BLK), F32)
        res_sum = jnp.zeros((width, BLK), F32)
        rate_sum = jnp.zeros((width, BLK), F32)
        for b in reversed(range(blocks)):
            at = slice(b * width, (b + 1) * width)
            rs_ref[g, at, :] = state
            first, second = sums_ref[g, at, :BLK], sums_ref[g, at, BLK:]
            before = states_ref[g, at, :]
            res_sum = res_sum + jnp.where(low, first * before, 0.0)
            rate_sum = rate_sum + (second + jnp.where(low, first, 0.0)) * before
            state, twin = (
                step * state + couple * twin + first,
                step * twin + jnp.where(low, 0.0, second),
            )
        fin_ref[g * width : (g + 1) * width, :] = state
        decay = jnp.exp(-rate_two[g : g + 1, :])
        cross_ref[0, g * width : (g + 1) * width, :] = decay * res_sum
        cross_ref[1, g * width : (g + 1) * width, :] = decay * rate_sum
    causal = rows((BLK, BLK)) >= lanes((BLK, BLK))
    for g in range(groups):
        own = slice(g * poles, (g + 1) * poles)
        y = stacked(gt_ref, g, width, blocks)
        taps = mm(
            jnp.concatenate([u_hi[own], u_hi[own], u_lo[own]], axis=0),
            jnp.concatenate([v_hi[own], v_lo[own], v_hi[own]], axis=0),
            0,
            0,
        )
        taps = jnp.where(causal, taps, 0.0).astype(BF16)
        out = with_states(y, taps, rs_ref[g], trail[0][own], trail[1][own])
        for b in range(blocks):
            bt_ref[g * width : (g + 1) * width, b * BLK : (b + 1) * BLK] = out[
                b * width : (b + 1) * width
            ]
        x = stacked(xt_ref, g, width, blocks)
        pairs = jnp.where(causal, mm(y, x, 0, 0), 0.0).astype(BF16)
        rhs = jnp.concatenate(
            [
                jnp.concatenate([v_hi[own], v_lo[own]], axis=1),
                jnp.concatenate([w_hi[own], w_lo[own]], axis=1),
                jnp.zeros((BLK - 2 * poles, 2 * BLK), BF16),
            ],
            axis=0,
        )
        held = mm(jnp.concatenate([pairs, pairs], axis=1), rhs, 1, 1)
        since = rows((BLK, BLK)) - 64.0
        held = held * jnp.exp(-rate_two[g : g + 1, :] * since)
        res_row = jnp.sum(jnp.where(low, held, 0.0), axis=0, keepdims=True)
        rate_row = jnp.sum(jnp.where(low, since * held, -held), axis=0, keepdims=True)
        one = slice(g * width, g * width + 1)
        cross_ref[0, one, :] = cross_ref[0, one, :] + res_row
        cross_ref[1, one, :] = cross_ref[1, one, :] + rate_row
    starts = fin_ref[...].T
    start, start_lag = starts[:poles], starts[poles : 2 * poles]
    state_in, slope_in = in_ref[:poles, :], in_ref[poles:, :]
    decay = jnp.exp(-by_channel(rate_ref[...], channels))
    res_cross = cross_ref[0].T[:poles]
    rate_cross = cross_ref[1].T
    res_sum = res_cross + decay * start * state_in
    rate_sum = (
        rate_cross[:poles]
        + rate_cross[poles : 2 * poles]
        + decay * ((start_lag + start) * state_in + start * slope_in)
    )
    both = exact(indicator(groups, channels), jnp.concatenate([res_sum, rate_sum], axis=0), 1, 1)
    both = jnp.concatenate([both, jnp.zeros((groups, BLK - 2 * poles), F32)], axis=1)
    pay_ref[:poles, :] = start
    pay_ref[poles:, :] = jnp.concatenate([both[: groups // 2], both[groups // 2 :]], axis=1)
    for b in range(blocks):
        at = slice(b * BLK, (b + 1) * BLK)
        back_ref[at, :] = bt_ref[:, at].T


def leave_kernel(
    here_ref, all_ref, back_ref, key_ref, value_ref, rate_ref, res_ref, dk_ref, dv_ref, dres_ref, drate_ref
):
    tokens, channels = back_ref.shape
    groups, poles = rate_ref.shape
    mine = 2 * here_ref[0] + here_ref[1]
    count = all_ref.shape[0]
    rate_nc = by_channel(rate_ref[...], channels)
    rate_row, res_row = by_column(rate_ref[...]).T, by_column(res_ref[...]).T
    state = jnp.zeros((poles, channels), F32)
    total = jnp.zeros((groups // 2, channels), F32)
    for place in range(count):
        gap = (place - 1 - mine).astype(F32)
        lag = jnp.maximum(gap, 0.0) * float(tokens)
        weight = jnp.where(gap >= 0.0, jnp.exp(-rate_nc * lag), 0.0)
        state = state + weight * all_ref[place, :poles, :]
        total = total + all_ref[place, poles:, :]
    tall = spread(state, groups)
    scale = 1.0 / float(tokens * count)
    both = jnp.concatenate([total[:, : 2 * poles], total[:, BLK : BLK + 2 * poles]], axis=0)
    dres_ref[...] = both[:, :poles] * scale
    drate_ref[...] = -res_ref[...] * both[:, poles:] * scale
    for b in range(tokens // BLK):
        at = slice(b * BLK, (b + 1) * BLK)
        time = float(tokens - b * BLK) - rows((BLK, groups * poles))
        trail = res_row * jnp.exp(-rate_row * time)
        back = back_ref[at, :] + modes(trail, tall)
        dk_ref[at, :] = (back * value_ref[at, :].astype(F32)).astype(BF16)
        dv_ref[at, :] = (back * key_ref[at, :].astype(F32)).astype(BF16)


def block_copies(z, refs, to_ref, sem):
    own, r1, l1, r2, l2, r3, l3, r4, l4 = refs
    half = r4.shape[0]
    whole = ((0, own), (-1, r1), (1, l1), (-2, r2), (2, l2), (-3, r3), (3, l3))
    nz = len(whole) + 1
    for far, ref in whole:
        at = lax.rem(z + far + nz, nz)
        yield at, ref, lambda slot: to_ref.at[slot], lambda slot: sem.at[slot, 0]
    at = lax.rem(z + nz // 2, nz)
    yield at, r4, lambda slot: to_ref.at[slot, pl.ds(0, half), :], lambda slot: sem.at[slot, 0]
    yield at, l4, lambda slot: to_ref.at[slot, pl.ds(half, half), :], lambda slot: sem.at[slot, 1]


def fetch_half(z, which, refs, half_ref, sem):
    count = half_ref.shape[0]
    far_slot = lax.rem(z + count, count)
    far_here = lax.div(lax.rem(z + count, 2 * count), count) == which
    for at, ref, place, signal in block_copies(z, refs, half_ref, sem):
        slot = lax.rem(at, count)

        @pl.when(lax.div(at, count) == which)
        def _():
            pltpu.make_async_copy(ref, place(slot), signal(slot)).start()

    def wait(j):
        split_here = jnp.logical_and(far_here, far_slot == j)
        tokens = half_ref.shape[1]

        @pl.when(split_here)
        def _():
            for part in range(2):
                piece = half_ref.at[j, pl.ds(part * (tokens // 2), tokens // 2), :]
                pltpu.make_async_copy(piece, piece, sem.at[j, part]).wait()

        @pl.when(jnp.logical_not(split_here))
        def _():
            pltpu.make_async_copy(half_ref.at[j], half_ref.at[j], sem.at[j, 0]).wait()

    return wait


def away_kernel(here_ref, *refs):
    blocks, gates, (away_ref, half_ref, sem) = refs[:9], refs[9:13], refs[13:]
    count, _, width = half_ref.shape
    wait = fetch_half(here_ref[2], 1 - here_ref[1], blocks, half_ref, sem)
    for j in range(count):
        wait(j)
        at = slice(j * width, (j + 1) * width)
        for i, gate in enumerate(gates):
            away_ref[i, :, at] = mm(gate[...], half_ref[j]).astype(BF16)


def project_kernel(here_ref, *refs):
    blocks, (mine_ref, other_ref), outs, (f_ref, w_ref, f_sem, w_sem) = refs[:9], refs[9:11], refs[11:15], refs[15:]
    core, z, x = here_ref[1], here_ref[2], here_ref[3]
    nz, tokens, _ = f_ref.shape
    nx, half, _ = mine_ref.shape
    feat = [
        pltpu.make_async_copy(ref, place(at), signal(at))
        for at, ref, place, signal in block_copies(z, blocks, f_ref, f_sem)
    ]
    order = (2, 1, 3, 0)
    weight = {}
    for i in order:
        at = lax.rem(x - i + nx, nx)
        weight[i] = [
            pltpu.make_async_copy(
                ref.at[at], w_ref.at[i, pl.ds(pl.multiple_of(first, half), half), :], w_sem.at[i, j]
            )
            for j, (ref, first) in enumerate(((mine_ref, core * half), (other_ref, (1 - core) * half)))
        ]
    for copy in weight[order[0]] + feat:
        copy.start()
    for i in order[1:]:
        for copy in weight[i]:
            copy.start()
    for copy in feat:
        copy.wait()
    tile = TILE
    for i in order:
        for copy in weight[i]:
            copy.wait()
        for m in range(tokens // tile):
            at = slice(m * tile, (m + 1) * tile)
            lhs = jnp.concatenate([f_ref[j, at, :] for j in range(nz)], axis=1)
            outs[i][at, :] = mm(lhs, w_ref[i]).astype(BF16)


def chip_kernel(here_ref, *refs):
    blocks, came_ref, gates, outs, (gate_ref, half_ref, sem) = refs[:9], refs[9], refs[10:14], refs[14:18], refs[18:]
    y, core = here_ref[0], here_ref[1]
    count, _, width = half_ref.shape
    wait = fetch_half(here_ref[2], core, blocks, half_ref, sem)
    for i, gate in enumerate(gates):
        gate_ref[i] = gate[...]
    for j in range(count):
        wait(j)
        at = slice(j * width, (j + 1) * width)
        for r, out in enumerate(outs):
            i = lax.rem(8 - y - r, 4)
            part = mm(gate_ref[i], half_ref[j])
            out[:, at] = (part + came_ref[i, :, at].astype(F32)).astype(BF16)


def column_kernel(a_ref, b_ref, c_ref, d_ref, out_ref):
    total = (a_ref[...].astype(F32) + b_ref[...].astype(F32)) + (
        c_ref[...].astype(F32) + d_ref[...].astype(F32)
    )
    out_ref[...] = total.astype(BF16)


def total_kernel(scale, in_ref, out_ref):
    for b in range(in_ref.shape[1] // BLK):
        at = slice(b * BLK, (b + 1) * BLK)
        out_ref[at, :] = in_ref[:, at].astype(F32).T * scale


MIB = 2**20


def call(kernel, outs, scratch, ops, vmem, us, scalars=0, far=()):
    spec = pl.BlockSpec(memory_space=pltpu.VMEM)
    return pl.pallas_call(
        kernel,
        out_shape=outs,
        in_specs=[
            pl.BlockSpec(memory_space=pltpu.SMEM)
            if i < scalars
            else (pl.BlockSpec(memory_space=pltpu.HBM) if i in far else spec)
            for i in range(len(ops))
        ],
        out_specs=[spec] * len(outs),
        scratch_shapes=scratch,
        compiler_params=pltpu.CompilerParams(vmem_limit_bytes=vmem * MIB),
        cost_estimate=pl.CostEstimate(
            flops=1000, bytes_accessed=int(us * 3.69e6), transcendentals=0
        ),
    )(*ops)


def shift(n, by):
    return [(i, (i + by) % n) for i in range(n)]


def gather_ctx(item):
    n = lax.axis_size(CTX)
    return lax.all_to_all(
        jnp.broadcast_to(item[None], (n,) + item.shape), CTX, split_axis=0, concat_axis=0
    )


def after(value, *others):
    return lax.optimization_barrier((value, others))[0]


def local(query, key, value, out_grad, out_weight, rate, residue):
    tokens, channels = query.shape
    groups, poles = rate.shape
    feats = out_weight.shape[0]
    y, core = lax.axis_index("y"), lax.axis_index("core")
    x, z = lax.axis_index("x"), lax.axis_index("z")
    nx, ny, nz = lax.axis_size("x"), lax.axis_size("y"), lax.axis_size("z")
    here = jnp.stack([y, core, z, x]).astype(jnp.int32)
    swap = [(0, 1), (1, 0)]
    sds = jax.ShapeDtypeStruct
    half_scratch = [
        pltpu.VMEM((nz // 2, tokens, channels), BF16),
        pltpu.SemaphoreType.DMA((nz // 2, 2)),
    ]
    stack_shape = (groups, tokens // BLK * (channels // groups))

    def both_ways(axis, pair):
        n = lax.axis_size(axis)
        return (
            lax.ppermute(pair[0], axis, shift(n, 1)),
            lax.ppermute(pair[1], axis, shift(n, -1)),
        )

    rows_x = feats // nx
    half_rows = rows_x // 2
    w_mine = lax.dynamic_index_in_dim(
        out_weight.reshape(nx, 2, half_rows, channels), core, 1, keepdims=False
    )
    w_mine = lax.all_to_all(w_mine, "x", split_axis=0, concat_axis=0)

    hop1 = both_ways("z", (out_grad, out_grad))

    conv_own, ends, xt, states = call(
        forward_kernel,
        [
            sds((tokens, channels), F32),
            sds((2 * poles, channels), F32),
            sds((channels, tokens), BF16),
            sds(stack_shape + (BLK,), F32),
        ],
        [
            pltpu.VMEM((channels, tokens), F32),
            pltpu.VMEM(stack_shape + (2 * BLK,), F32),
            pltpu.VMEM((channels, BLK), F32),
        ],
        [key, value, rate, residue],
        12,
        10.0,
    )
    other_ends = lax.ppermute(ends, "core", swap)
    pair = jnp.stack([ends, other_ends])
    hop2 = both_ways("z", after(hop1, ends))
    all_ends = [ends, other_ends] + [
        lax.ppermute(pair, "y", shift(ny, i)) for i in range(1, ny)
    ]
    conv, gated, entering = call(
        enter_kernel,
        [
            sds((tokens, channels), F32),
            sds((channels, tokens), BF16),
            sds((2 * poles, channels), F32),
        ],
        [],
        [here] + all_ends + [after(conv_own, hop2), query, rate, residue],
        8,
        10.0,
        scalars=1,
    )
    hop3 = both_ways("z", after(hop2, all_ends))
    w_other = lax.ppermute(after(w_mine, hop2, all_ends), "core", swap)
    gates = [gated] + [lax.ppermute(gated, "x", shift(nx, i)) for i in range(1, nx)]
    right, left = after(hop3, gated)
    hop4 = both_ways("z", (right[: tokens // 2], left[tokens // 2 :]))
    blocks = [out_grad, *hop1, *hop2, *hop3, *hop4]

    own, one, two, three = call(
        project_kernel,
        [sds((tokens, channels), BF16)] * nx,
        [
            pltpu.VMEM((nz, tokens, channels), BF16),
            pltpu.VMEM((nx, rows_x, channels), BF16),
            pltpu.SemaphoreType.DMA((nz, 2)),
            pltpu.SemaphoreType.DMA((nx, 2)),
        ],
        [here] + blocks + [w_mine, w_other],
        16,
        6.0,
        scalars=1,
        far=tuple(range(1, 12)),
    )
    sums = [
        lax.ppermute(part, "x", shift(nx, -i)) for i, part in ((2, two), (1, one), (3, three))
    ]

    (away,) = call(
        away_kernel,
        [sds((nx, channels, half_rows), BF16)],
        half_scratch,
        [here] + after(blocks, own) + gates,
        12,
        0.5,
        scalars=1,
        far=tuple(range(1, 10)),
    )
    came = lax.ppermute(away, "core", swap)

    chip = call(
        chip_kernel,
        [sds((channels, half_rows), BF16)] * nx,
        [pltpu.VMEM((nx, channels, tokens), BF16)] + half_scratch,
        [here] + blocks + [came] + gates,
        16,
        0.5,
        scalars=1,
        far=tuple(range(1, 10)),
    )
    parts = [chip[0]] + [lax.ppermute(chip[r], "y", shift(ny, r)) for r in range(1, ny)]
    d_query, back_own, pay = call(
        backward_kernel,
        [
            sds((tokens, channels), BF16),
            sds((tokens, channels), F32),
            sds((poles + groups // 2, channels), F32),
        ],
        [
            pltpu.VMEM((channels, tokens), BF16),
            pltpu.VMEM((channels, tokens), F32),
            pltpu.VMEM(stack_shape + (2 * BLK,), F32),
            pltpu.VMEM(stack_shape + (BLK,), F32),
            pltpu.VMEM((channels, BLK), F32),
            pltpu.VMEM((2, channels, BLK), F32),
        ],
        [after(own, chip)] + sums + [query, conv, xt, states, entering, rate, residue],
        16,
        20.0,
    )
    parts[0] = after(parts[0], pay)
    (column,) = call(column_kernel, [sds((channels, half_rows), BF16)], [], parts, 8, 1.0)
    all_pay = gather_ctx(pay)
    route = [(a * nx + b, b * nx + (a + b) % nx) for a in range(ny) for b in range(nx)]
    column = lax.ppermute(column, ("y", "x"), route)

    d_key, d_value, d_residue, d_rate = call(
        leave_kernel,
        [
            sds((tokens, channels), BF16),
            sds((tokens, channels), BF16),
            sds((groups, poles), F32),
            sds((groups, poles), F32),
        ],
        [],
        [here, all_pay, back_own, key, value, rate, residue],
        8,
        2.5,
        scalars=1,
    )
    (d_weight,) = call(
        functools.partial(total_kernel, 1.0 / float(tokens * 2 * nx)),
        [sds((half_rows, channels), F32)],
        [],
        [column],
        8,
        1.5,
    )
    return (d_query, d_key, d_value, d_weight, d_residue, d_rate)


def solution(mesh):
    fine = Mesh(mesh.devices.reshape(4, 2, 4, 8), ("y", "core", "x", "z"))
    both = P(CTX, CHAN)
    param = P(CHAN, None)
    return jax.shard_map(
        local,
        mesh=fine,
        in_specs=(both, both, both, both, P(None, CHAN), param, param),
        out_specs=(both, both, both, both, param, param),
        check_vma=False,
    )
```
